32 devices in a mesh: parts: 2 (over x), space: 8 (over z, y), chan: 2 (over core).
Axes of the slice: x: 2, y: 2, z: 4, core: 2. Of those that a mesh axis runs over, the one named last changes fastest.
Arguments:
- field: bfloat16 [192, 768, 256], P(('parts', 'space'), None, 'chan'), parts along dimension 0, may hold values from -6 to 6
- spectral_weight: bfloat16 [96, 256, 256], P('space', None, 'chan'), may hold values from -5 to 5
- cotangent: bfloat16 [192, 768, 256], P(('parts', 'space'), None, 'chan'), parts along dimension 0, may hold values from -6 to 6
Outputs:
- output: bfloat16 [192, 768, 256], P(('parts', 'space'), None, 'chan'), parts along dimension 0
- field_grad: bfloat16 [192, 768, 256], P(('parts', 'space'), None, 'chan'), parts along dimension 0
- weight_grad: bfloat16 [192, 256, 256], P(('parts', 'space'), None, 'chan'), parts along dimension 0
The draws below stay inside these ranges and needn't reach their ends.
There are 2 independent parts, one for each index of `parts`. The reference program is written for one: setup_inputs(seed, part) draws one part's arguments, and reference() takes and returns one part's arrays. A program takes and returns all parts, laid end to end along the dimension named above; an argument that names none is the same for every part. Nothing has to cross between parts.
All inputs are finite; a program needn't handle non-finite values.
Results may differ from the reference program's by a relative error of at most 0.02.
Values may be sent and summed in bfloat16 or wider, within the bound.
A program may use at most 128 MiB of HBM per device.

```python
import math
import jax
import jax.numpy as jnp
from jax import lax

CH = 256
NLON = 768
LMAX = 96
NLAT = 96


def shard_levels(stream_key, extent, cuts, smallest, high):
    def one(axis_at, parts):
        draws = jax.random.uniform(jax.random.fold_in(jax.random.fold_in(stream_key, 6), axis_at), (parts,), jnp.float32, smallest / len(cuts), high / len(cuts))
        return jnp.repeat(jnp.exp(draws), extent[axis_at] // parts).reshape((-1,) + (1,) * (len(extent) - axis_at - 1))

    factor_of = one(*cuts[0])
    for cut in cuts[1:]:
        factor_of = factor_of * one(*cut)
    return factor_of


def scatter_about(own_key, dims, deviation, limit, cuts=(), kind=jnp.bfloat16):
    result = jax.random.normal(own_key, dims, jnp.float32) * deviation
    if len(cuts) > 0:
        result = shard_levels(own_key, dims, cuts, -0.22, 0.18) * result
    return jnp.clip(result, min=-limit, max=limit).astype(kind)


def setup_inputs(seed: int = 0, part: int = 0) -> dict:
    key_of = jax.random.split(jax.random.key(seed), 4)
    part_splits = jax.random.split(jax.random.fold_in(key_of[3], part), 4)
    field = scatter_about(part_splits[0], (NLAT, NLON, CH), 1.0, 6.0, ((0, 8), (2, 2)))
    spectral_weight = scatter_about(key_of[1], (LMAX, CH, CH), 1.0, 5.0, ((0, 8), (2, 2)))
    cotangent = scatter_about(part_splits[2], (NLAT, NLON, CH), 1.0, 6.0, ((0, 8), (2, 2)))
    return dict(field=field, spectral_weight=spectral_weight, cotangent=cotangent)


LIMIT = 2.0 ** 40
SHRINK = 2.0 ** (-40)
LOGSTEP = 40.0 * math.log(2.0)

def stored(values):
    return lax.optimization_barrier(values.astype(jnp.bfloat16))

def legendre(order_ints, cosines, sine_values, degrees):
    orders = order_ints.astype(jnp.float32)
    order_col = orders[:, None]
    log_start = 0.5 * (jnp.log((2.0 * order_col + 1.0) / (4.0 * math.pi)) + lax.lgamma(order_col + 0.5) - lax.lgamma(order_col + 1.0) - 0.5 * math.log(math.pi)) + order_col * jnp.log(sine_values)[None, :]
    state_shape = (orders.shape[0], cosines.shape[0])
    degree_list = jnp.arange(degrees).astype(jnp.float32)
    degree_col = degree_list[:, None]
    order_row = orders[None, :]
    upper_all = jnp.sqrt((4.0 * degree_col * degree_col - 1.0) / jnp.maximum(degree_col * degree_col - order_row * order_row, 1.0))
    lower_deg = degree_col - 1.0
    lower_all = jnp.sqrt(jnp.maximum(lower_deg * lower_deg - order_row * order_row, 0.0) / jnp.maximum(4.0 * lower_deg * lower_deg - 1.0, 1.0))

    def advance(state_now, inputs):
        previous, before, rescales = state_now
        degree, upper_row, lower_row = inputs
        upper_coef = upper_row[:, None]
        lower_coef = lower_row[:, None]
        newest = jnp.where(degree == order_col, 1.0, jnp.where(degree > order_col, upper_coef * (cosines[None, :] * previous - lower_coef * before), 0.0))
        too_large = jnp.abs(newest) > LIMIT
        newest = jnp.where(too_large, newest * SHRINK, newest)
        previous = jnp.where(too_large, previous * SHRINK, previous)
        rescales = rescales + too_large.astype(jnp.float32)
        return ((newest, previous, rescales), newest * jnp.exp(log_start + rescales * LOGSTEP))
    zero_state = jnp.zeros(state_shape, jnp.float32)
    final_state, values = lax.scan(advance, (zero_state, zero_state, zero_state), (degree_list, upper_all, lower_all), unroll=16)
    return jnp.transpose(values, (1, 2, 0))

def spectral_tables(order_ints, latitudes, longitudes, degrees):
    half_lats = latitudes // 2
    latitude = (jnp.arange(latitudes).astype(jnp.float32) + 0.5) * (math.pi / latitudes)
    sine_values = jnp.sin(latitude)
    north_angle = latitude[:half_lats]
    north = legendre(order_ints, jnp.cos(north_angle), jnp.sin(north_angle), degrees)
    parity = (order_ints.astype(jnp.int32)[:, None] + jnp.arange(degrees, dtype=jnp.int32)[None, :]) % 2
    signs = (1 - 2 * parity).astype(jnp.float32)
    south = signs[:, None, :] * north[:, ::-1, :]
    base_values = jnp.concatenate([north, south], axis=1)
    quadrature = math.pi ** 1.5 / math.sqrt(latitudes * longitudes) * sine_values
    analysis = quadrature[None, :, None] * base_values
    synthesis = math.sqrt(4.0 * math.pi / (latitudes * longitudes)) * base_values
    return (analysis, synthesis)

def fourier_table(longitudes, order_total):
    columns = jnp.arange(longitudes, dtype=jnp.int32)[:, None] * jnp.arange(order_total, dtype=jnp.int32)[None, :]
    phase_angle = 2.0 * math.pi / longitudes * (columns % longitudes).astype(jnp.float32)
    columns_table = jnp.stack([jnp.cos(phase_angle), -jnp.sin(phase_angle)], axis=2)
    return columns_table.reshape(longitudes, 2 * order_total)

def order_weights(order_total):
    return jnp.repeat(jnp.where(jnp.arange(order_total) == 0, 1.0, 2.0), 2).astype(jnp.float32)

def reference(field, spectral_weight, cotangent):
    mix_scale = 1.0 / math.sqrt(CH)
    forward_table = fourier_table(NLON, LMAX)
    forward_cast = stored(forward_table).astype(jnp.float32)
    inverse_cast = stored((forward_table * order_weights(LMAX)[None, :]).T).astype(jnp.float32)
    analysis, synthesis = spectral_tables(jnp.arange(LMAX, dtype=jnp.int32), NLAT, NLON, LMAX)
    analysis_cast = stored(analysis).astype(jnp.float32)
    synthesis_cast = stored(synthesis).astype(jnp.float32)
    weight_wide = spectral_weight.astype(jnp.float32)
    field_wide = field.astype(jnp.float32)
    cotangent_wide = cotangent.astype(jnp.float32)
    fourier = stored(jnp.einsum('jkc,kn->jnc', field_wide, forward_cast)).astype(jnp.float32)
    coeffs = stored(jnp.einsum('mjl,jmrc->mlrc', analysis_cast, fourier.reshape(NLAT, LMAX, 2, CH))).astype(jnp.float32)
    mixed_coef = stored(jnp.einsum('mlrc,lco->mlro', coeffs, weight_wide) * mix_scale).astype(jnp.float32)
    grid_values = stored(jnp.einsum('mjl,mlrc->jmrc', synthesis_cast, mixed_coef)).astype(jnp.float32).reshape(NLAT, 2 * LMAX, CH)
    response = jnp.einsum('jnc,nk->jkc', grid_values, inverse_cast)
    normal_cdf = 0.5 * (1.0 + lax.erf(response * (1.0 / math.sqrt(2.0))))
    output = (field_wide + response * normal_cdf).astype(jnp.bfloat16)
    density = jnp.exp(-0.5 * response * response) * (1.0 / math.sqrt(2.0 * math.pi))
    response_grad = stored(cotangent_wide * (normal_cdf + response * density)).astype(jnp.float32)
    grid_grad = stored(jnp.einsum('jkc,nk->jnc', response_grad, inverse_cast)).astype(jnp.float32)
    mixed_grad = stored(jnp.einsum('mjl,jmrc->mlrc', synthesis_cast, grid_grad.reshape(NLAT, LMAX, 2, CH))).astype(jnp.float32)
    weight_grad = (jnp.einsum('mlrc,mlro->lco', coeffs, mixed_grad) * mix_scale).astype(jnp.bfloat16)
    coeff_grad = stored(jnp.einsum('mlro,lco->mlrc', mixed_grad, weight_wide) * mix_scale).astype(jnp.float32)
    fourier_grad = stored(jnp.einsum('mjl,mlrc->jmrc', analysis_cast, coeff_grad)).astype(jnp.float32).reshape(NLAT, 2 * LMAX, CH)
    field_grad = (cotangent_wide + jnp.einsum('jnc,kn->jkc', fourier_grad, forward_cast)).astype(jnp.bfloat16)
    return (output, field_grad, weight_grad)
```

```python
import functools
import math

import jax
import jax.numpy as jnp
import ml_dtypes
import numpy as np
from jax import lax
from jax.experimental import pallas as pl
from jax.experimental.pallas import tpu as pltpu
from jax.sharding import PartitionSpec as P

LIMIT = 2.0**40
SHRINK = 2.0 ** (-40)
LOGSTEP = 40.0 * math.log(2.0)
MESH = pl.DeviceIdType.MESH


def fourier_tables(longitudes, order_list):
    products = (np.asarray(order_list)[:, None] * np.arange(longitudes)[None, :]) % longitudes
    angle = 2.0 * math.pi / longitudes * products
    table = np.stack([np.cos(angle), -np.sin(angle)], axis=1)
    weights = np.where(np.asarray(order_list) == 0, 1.0, 2.0)[:, None, None]
    forward = table.reshape(-1, longitudes).astype(np.float32)
    inverse = (table * weights).reshape(-1, longitudes).astype(np.float32)
    return forward.astype(ml_dtypes.bfloat16), inverse.astype(ml_dtypes.bfloat16)


def latitude_rows(latitudes, longitudes, orders):
    half = latitudes // 2
    north = (np.arange(half) + 0.5) * (math.pi / latitudes)
    cosines = np.concatenate([np.cos(north), -np.cos(north)[::-1]])
    sines = np.concatenate([np.sin(north), np.sin(north)[::-1]])
    order = np.arange(orders)
    gammas = np.array([math.lgamma(m + 0.5) - math.lgamma(m + 1.0) for m in order])
    start = 0.5 * (np.log((2.0 * order + 1.0) / (4.0 * math.pi)) + gammas - 0.5 * math.log(math.pi))
    log_start = start[:, None] + order[:, None] * np.log(sines)[None, :]
    area = latitudes * longitudes
    rows = np.stack([cosines, math.pi**1.5 / math.sqrt(area) * sines])
    return (
        log_start.astype(np.float32),
        rows.astype(np.float32),
        math.sqrt(4.0 * math.pi / area),
    )


def legendre_into(log_start, rows, synthesis_scale, first_order, values, analysis, synthesis):
    held, degrees, latitudes = values.shape
    shape = (held, latitudes)
    order = (lax.broadcasted_iota(jnp.int32, shape, 0) + first_order).astype(jnp.float32)
    cosines = jnp.broadcast_to(rows[0:1, :], shape)
    start = log_start[...]

    def step(at, state):
        previous, before, rescales = state
        degree = at.astype(jnp.float32)
        lower_deg = degree - 1.0
        square = order * order
        upper = jnp.sqrt((4.0 * degree * degree - 1.0) / jnp.maximum(degree * degree - square, 1.0))
        lower = jnp.sqrt(
            jnp.maximum(lower_deg * lower_deg - square, 0.0)
            / jnp.maximum(4.0 * lower_deg * lower_deg - 1.0, 1.0)
        )
        newest = jnp.where(
            degree == order,
            1.0,
            jnp.where(degree > order, upper * (cosines * previous - lower * before), 0.0),
        )
        too_large = jnp.abs(newest) > LIMIT
        newest = jnp.where(too_large, newest * SHRINK, newest)
        previous = jnp.where(too_large, previous * SHRINK, previous)
        rescales = rescales + jnp.where(too_large, 1.0, 0.0)
        values[:, pl.ds(at, 1), :] = (newest * jnp.exp(start + rescales * LOGSTEP))[:, None, :]
        return newest, previous, rescales

    zero = jnp.zeros(shape, jnp.float32)
    lax.fori_loop(0, degrees, step, (zero, zero, zero))
    quadrature = rows[1:2, :]

    def finish(m, carry):
        analysis[m] = (values[m] * quadrature).astype(jnp.bfloat16)
        synthesis[m] = (values[m] * synthesis_scale).astype(jnp.bfloat16)
        return carry

    lax.fori_loop(0, held, finish, 0)


class Exchange:
    def __init__(self, n, held, spread, sparse):
        self.n, self.held, self.spread, self.sparse = n, held, spread, sparse

    def greet(self, chan):
        me = lax.axis_index("space")
        barrier = pltpu.get_barrier_semaphore()
        for k in range(1, self.n):
            pl.semaphore_signal(
                barrier, inc=1, device_id={"space": lax.rem(me + k, self.n)}, device_id_type=MESH
            )
        if chan:
            pl.semaphore_signal(
                barrier, inc=1, device_id={"chan": 1 - lax.axis_index("chan")}, device_id_type=MESH
            )
        pl.semaphore_wait(barrier, self.n - 1 + (1 if chan else 0))

    def source(self, x, d):
        return x.at[:, d] if self.spread else x.at[pl.ds(d * self.held, self.held)]

    def slot(self, y, s):
        return y.at[pl.ds(s * self.held, self.held)] if self.spread else y.at[:, s]

    def when(self, other, run):
        if self.sparse:
            pl.when(lax.axis_index("space") + other >= self.n - 1)(run)
        else:
            run()

    def copy(self, x, y, k, send_sem, recv_sem, sending):
        me = lax.axis_index("space")
        other = lax.rem(me + k, self.n) if sending else lax.rem(me + self.n - k, self.n)
        return other, pltpu.make_async_remote_copy(
            src_ref=self.source(x, other),
            dst_ref=self.slot(y, me if sending else other),
            send_sem=send_sem.at[k],
            recv_sem=recv_sem.at[k],
            device_id={"space": other},
            device_id_type=MESH,
        )


def send_all(ex, x, y, send_sem, recv_sem):
    for k in range(1, ex.n):
        other, copy = ex.copy(x, y, k, send_sem, recv_sem, True)
        ex.when(other, copy.start)


def wait_sends(ex, x, y, send_sem, recv_sem):
    for k in range(1, ex.n):
        other, copy = ex.copy(x, y, k, send_sem, recv_sem, True)
        ex.when(other, copy.wait_send)


def zero_fill(ex, targets, zero, zero_sem, start):
    me = lax.axis_index("space")
    for k in range(ex.n):
        other = lax.rem(me + ex.n - k, ex.n)

        @pl.when(me + other < ex.n - 1)
        def _():
            for i, y in enumerate(targets):
                copy = pltpu.make_async_copy(zero, ex.slot(y, other), zero_sem.at[i, k])
                copy.start() if start else copy.wait()


def plain_kernel(ex, legendre, *refs):
    if legendre is not None:
        x, log_start, rows, y, analysis, synthesis, values = refs[:7]
        send_sem, recv_sem, own_sem = refs[7:]
    elif ex.sparse:
        x, y, zero, zero_sem, send_sem, recv_sem, own_sem = refs
    else:
        x, y, send_sem, recv_sem, own_sem = refs
    me = lax.axis_index("space")
    ex.greet(False)
    send_all(ex, x, y, send_sem, recv_sem)
    own = pltpu.make_async_copy(ex.source(x, me), ex.slot(y, me), own_sem)
    ex.when(me, own.start)
    if ex.sparse:
        zero[...] = jnp.zeros_like(zero)
        zero_fill(ex, [y], zero, zero_sem, True)
    if legendre is not None:
        first_order = (ex.n - 1 - me) * ex.held
        legendre_into(log_start, rows, legendre, first_order, values, analysis, synthesis)
    ex.when(me, own.wait)
    for k in range(1, ex.n):
        other, copy = ex.copy(x, y, k, send_sem, recv_sem, False)
        ex.when(other, copy.wait_recv)
    wait_sends(ex, x, y, send_sem, recv_sem)
    if ex.sparse:
        zero_fill(ex, [y], zero, zero_sem, False)


def gather_kernel(ex, by_channel, x, y, zero, zero_sem, send_sem, recv_sem, own_sem, fsend, frecv):
    me = lax.axis_index("space")
    chan = lax.axis_index("chan")
    mine = y.at[chan] if by_channel else y.at[0]
    theirs = y.at[chan] if by_channel else y.at[1]
    coming = y.at[1 - chan] if by_channel else y.at[1]
    ex.greet(True)
    send_all(ex, x, mine, send_sem, recv_sem)

    def forward(k, other, source):
        return pltpu.make_async_remote_copy(
            src_ref=source,
            dst_ref=ex.slot(theirs, other),
            send_sem=fsend.at[k],
            recv_sem=frecv.at[k],
            device_id={"chan": 1 - chan},
            device_id_type=MESH,
        )

    own = pltpu.make_async_copy(ex.source(x, me), ex.slot(mine, me), own_sem)
    ex.when(me, own.start)
    ex.when(me, forward(0, me, ex.source(x, me)).start)
    zero[...] = jnp.zeros_like(zero)
    zero_fill(ex, [y.at[0], y.at[1]], zero, zero_sem, True)
    for k in range(1, ex.n):
        other, copy = ex.copy(x, mine, k, send_sem, recv_sem, False)

        def pass_on(copy=copy, k=k, other=other):
            copy.wait_recv()
            forward(k, other, ex.slot(mine, other)).start()

        ex.when(other, pass_on)
    ex.when(me, own.wait)
    for k in range(ex.n):
        other = lax.rem(me + ex.n - k, ex.n)

        def settle(k=k, other=other):
            copy = pltpu.make_async_remote_copy(
                src_ref=ex.slot(mine, other),
                dst_ref=ex.slot(coming, other),
                send_sem=fsend.at[k],
                recv_sem=frecv.at[k],
                device_id={"chan": 1 - chan},
                device_id_type=MESH,
            )
            copy.wait_recv()
            copy.wait_send()

        ex.when(other, settle)
    wait_sends(ex, x, mine, send_sem, recv_sem)
    zero_fill(ex, [y.at[0], y.at[1]], zero, zero_sem, False)


def any_spec():
    return pl.BlockSpec(memory_space=pl.ANY)


def vmem_spec():
    return pl.BlockSpec(memory_space=pltpu.VMEM)


def params(collective_id):
    return pltpu.CompilerParams(
        collective_id=collective_id, has_side_effects=True, vmem_limit_bytes=24 * 2**20
    )


def swap(x, n, spread, sparse, collective_id, legendre=None):
    if spread:
        held, _, rows, width = x.shape
        shape = (n * held, rows, width)
    else:
        total, rows, width = x.shape
        held = total // n
        shape = (held, n, rows, width)
    ex = Exchange(n, held, spread, sparse)
    sems = [
        pltpu.SemaphoreType.DMA((n,)),
        pltpu.SemaphoreType.DMA((n,)),
        pltpu.SemaphoreType.DMA,
    ]
    out = jax.ShapeDtypeStruct(shape, x.dtype)
    if legendre is not None:
        log_start, rows_in, scale = legendre
        orders, latitudes = log_start.shape
        table = jax.ShapeDtypeStruct((orders, n * held, latitudes), jnp.bfloat16)
        return pl.pallas_call(
            functools.partial(plain_kernel, ex, scale),
            out_shape=(out, table, table),
            in_specs=[any_spec(), vmem_spec(), vmem_spec()],
            out_specs=(any_spec(), vmem_spec(), vmem_spec()),
            scratch_shapes=[pltpu.VMEM((orders, n * held, latitudes), jnp.float32)] + sems,
            compiler_params=params(collective_id),
            name="exchange_and_legendre",
        )(x, log_start, rows_in)
    scratch = list(sems)
    if sparse:
        zeros = [pltpu.VMEM((held, rows, width), x.dtype), pltpu.SemaphoreType.DMA((1, n))]
        scratch = zeros + scratch
    return pl.pallas_call(
        functools.partial(plain_kernel, ex, None),
        out_shape=out,
        in_specs=[any_spec()],
        out_specs=any_spec(),
        scratch_shapes=scratch,
        compiler_params=params(collective_id),
        name="exchange",
    )(x)


def swap_gather(x, n, by_channel, collective_id):
    total, rows, width = x.shape
    held = total // n
    ex = Exchange(n, held, False, True)
    return pl.pallas_call(
        functools.partial(gather_kernel, ex, by_channel),
        out_shape=jax.ShapeDtypeStruct((2, held, n, rows, width), x.dtype),
        in_specs=[any_spec()],
        out_specs=any_spec(),
        scratch_shapes=[
            pltpu.VMEM((held, rows, width), x.dtype),
            pltpu.SemaphoreType.DMA((2, n)),
            pltpu.SemaphoreType.DMA((n,)),
            pltpu.SemaphoreType.DMA((n,)),
            pltpu.SemaphoreType.DMA,
            pltpu.SemaphoreType.DMA((n,)),
            pltpu.SemaphoreType.DMA((n,)),
        ],
        compiler_params=params(collective_id),
        name="exchange_and_gather",
    )(x)


def dot32(formula, left, right):
    return jnp.einsum(formula, left, right, preferred_element_type=jnp.float32)


def local(field, spectral_weight, cotangent):
    n = lax.axis_size("space")
    held, longitudes, half = field.shape
    degrees_held, channels, _ = spectral_weight.shape
    latitudes = held * n
    degrees = degrees_held * n
    orders_held = degrees_held
    rows = 2 * orders_held
    mix_scale = 1.0 / math.sqrt(channels)
    chan = lax.axis_index("chan")
    block = n - 1 - lax.axis_index("space")
    order_list = np.arange(degrees).reshape(n, orders_held)[::-1].reshape(-1)
    forward_np, inverse_np = fourier_tables(longitudes, order_list)
    forward, inverse = jnp.asarray(forward_np), jnp.asarray(inverse_np)
    log_np, rows_np, scale = latitude_rows(latitudes, longitudes, degrees)
    log_start = lax.dynamic_slice_in_dim(jnp.asarray(log_np), block * orders_held, orders_held, 0)

    weight_halves = spectral_weight.reshape(degrees_held, 2, half, half)
    weight_own = lax.dynamic_index_in_dim(weight_halves, chan, 1, keepdims=False)
    weight_give = lax.dynamic_index_in_dim(weight_halves, 1 - chan, 1, keepdims=False)
    weight_other = lax.ppermute(weight_give, "chan", [(0, 1), (1, 0)])

    fourier = dot32("jkc,nk->jnc", field, forward).astype(jnp.bfloat16)
    by_order, analysis, synthesis = swap(
        fourier.reshape(held, n, rows, half),
        n,
        True,
        False,
        0,
        (log_start, jnp.asarray(rows_np), scale),
    )

    def to_degrees(table, values):
        values = values.reshape(latitudes, orders_held, 2, half)
        out = dot32("mlj,jmrc->lmrc", table, values).astype(jnp.bfloat16)
        return out.reshape(degrees, rows, half)

    def to_latitudes(table, values):
        values = values.reshape(degrees, orders_held, 2, half)
        out = dot32("mlj,lmrc->jmrc", table, values).astype(jnp.bfloat16)
        return out.reshape(latitudes, rows, half)

    coeffs = swap_gather(to_degrees(analysis, by_order), n, True, 1)
    coeffs = coeffs.reshape(2, degrees_held, n * rows, half)
    mixed = (
        dot32("lqc,lco->lqo", coeffs[0], weight_halves[:, 0])
        + dot32("lqc,lco->lqo", coeffs[1], weight_halves[:, 1])
    ) * mix_scale
    mixed = mixed.astype(jnp.bfloat16).reshape(degrees_held, n, rows, half)
    mixed_orders = swap(mixed, n, True, True, 2)
    grid = swap(to_latitudes(synthesis, mixed_orders), n, False, False, 3)
    grid = grid.reshape(held, n * rows, half)
    response = dot32("jnc,nk->jkc", grid, inverse)
    normal_cdf = 0.5 * (1.0 + lax.erf(response * (1.0 / math.sqrt(2.0))))
    output = (field.astype(jnp.float32) + response * normal_cdf).astype(jnp.bfloat16)
    density = jnp.exp(-0.5 * response * response) * (1.0 / math.sqrt(2.0 * math.pi))
    response_grad = (cotangent.astype(jnp.float32) * (normal_cdf + response * density)).astype(
        jnp.bfloat16
    )
    grid_grad = dot32("jkc,nk->jnc", response_grad, inverse).astype(jnp.bfloat16)
    grad_by_order = swap(grid_grad.reshape(held, n, rows, half), n, True, False, 4)
    grads = swap_gather(to_degrees(synthesis, grad_by_order), n, False, 5)
    grads = grads.reshape(2, degrees_held, n * rows, half)
    coeff_grad = (
        dot32("lqo,lco->lqc", grads[0], weight_own) + dot32("lqo,lco->lqc", grads[1], weight_other)
    ) * mix_scale
    coeff_grad = coeff_grad.astype(jnp.bfloat16).reshape(degrees_held, n, rows, half)
    coeff_orders = swap(coeff_grad, n, True, True, 6)
    fourier_band = swap(to_latitudes(analysis, coeff_orders), n, False, False, 7)
    fourier_band = fourier_band.reshape(held, n * rows, half)
    weight_grad = (dot32("xlqc,lqo->lxco", coeffs, grads[0]) * mix_scale).astype(jnp.bfloat16)
    field_grad = (
        cotangent.astype(jnp.float32) + dot32("jnc,nk->jkc", fourier_band, forward)
    ).astype(jnp.bfloat16)
    return (output, field_grad, weight_grad.reshape(degrees_held, channels, half))


def solution(mesh):
    in_specs = (
        P(("parts", "space"), None, "chan"),
        P("space", None, "chan"),
        P(("parts", "space"), None, "chan"),
    )
    out_specs = (
        P(("parts", "space"), None, "chan"),
        P(("parts", "space"), None, "chan"),
        P(("parts", "space"), None, "chan"),
    )
    return jax.shard_map(local, mesh=mesh, in_specs=in_specs, out_specs=out_specs, check_vma=False)
```

```python
import functools
import math

import jax
import jax.numpy as jnp
import ml_dtypes
import numpy as np
from jax import lax
from jax.experimental import pallas as pl
from jax.experimental.pallas import tpu as pltpu
from jax.sharding import PartitionSpec as P

LIMIT = 2.0**40
SHRINK = 2.0 ** (-40)
LOGSTEP = 40.0 * math.log(2.0)
MESH = pl.DeviceIdType.MESH


def fourier_tables(longitudes, order_list):
    products = (np.asarray(order_list)[:, None] * np.arange(longitudes)[None, :]) % longitudes
    angle = 2.0 * math.pi / longitudes * products
    table = np.stack([np.cos(angle), -np.sin(angle)], axis=1)
    weights = np.where(np.asarray(order_list) == 0, 1.0, 2.0)[:, None, None]
    forward = table.reshape(-1, longitudes).astype(np.float32)
    inverse = (table * weights).reshape(-1, longitudes).astype(np.float32)
    return forward.astype(ml_dtypes.bfloat16), inverse.astype(ml_dtypes.bfloat16)


def latitude_rows(latitudes, longitudes, orders):
    half = latitudes // 2
    north = (np.arange(half) + 0.5) * (math.pi / latitudes)
    cosines = np.concatenate([np.cos(north), -np.cos(north)[::-1]])
    sines = np.concatenate([np.sin(north), np.sin(north)[::-1]])
    order = np.arange(orders)
    gammas = np.array([math.lgamma(m + 0.5) - math.lgamma(m + 1.0) for m in order])
    start = 0.5 * (np.log((2.0 * order + 1.0) / (4.0 * math.pi)) + gammas - 0.5 * math.log(math.pi))
    log_start = start[:, None] + order[:, None] * np.log(sines)[None, :]
    area = latitudes * longitudes
    rows = np.stack([cosines, math.pi**1.5 / math.sqrt(area) * sines])
    return (
        log_start.astype(np.float32),
        rows.astype(np.float32),
        math.sqrt(4.0 * math.pi / area),
    )


def legendre_into(log_start, rows, synthesis_scale, first_order, values, analysis, synthesis):
    held, degrees, latitudes = values.shape
    shape = (held, latitudes)
    order = (lax.broadcasted_iota(jnp.int32, shape, 0) + first_order).astype(jnp.float32)
    cosines = jnp.broadcast_to(rows[0:1, :], shape)
    start = log_start[...]

    def step(at, state):
        previous, before, rescales = state
        degree = at.astype(jnp.float32)
        lower_deg = degree - 1.0
        square = order * order
        upper = jnp.sqrt((4.0 * degree * degree - 1.0) / jnp.maximum(degree * degree - square, 1.0))
        lower = jnp.sqrt(
            jnp.maximum(lower_deg * lower_deg - square, 0.0)
            / jnp.maximum(4.0 * lower_deg * lower_deg - 1.0, 1.0)
        )
        newest = jnp.where(
            degree == order,
            1.0,
            jnp.where(degree > order, upper * (cosines * previous - lower * before), 0.0),
        )
        too_large = jnp.abs(newest) > LIMIT
        newest = jnp.where(too_large, newest * SHRINK, newest)
        previous = jnp.where(too_large, previous * SHRINK, previous)
        rescales = rescales + jnp.where(too_large, 1.0, 0.0)
        values[:, pl.ds(at, 1), :] = (newest * jnp.exp(start + rescales * LOGSTEP))[:, None, :]
        return newest, previous, rescales

    zero = jnp.zeros(shape, jnp.float32)
    lax.fori_loop(0, degrees, step, (zero, zero, zero))
    quadrature = rows[1:2, :]

    def finish(m, carry):
        analysis[m] = (values[m] * quadrature).astype(jnp.bfloat16)
        synthesis[m] = (values[m] * synthesis_scale).astype(jnp.bfloat16)
        return carry

    lax.fori_loop(0, held, finish, 0)


class Exchange:
    def __init__(self, n, held, spread, sparse):
        self.n, self.held, self.spread, self.sparse = n, held, spread, sparse

    def greet(self, chan):
        me = lax.axis_index("space")
        barrier = pltpu.get_barrier_semaphore()
        for k in range(1, self.n):
            pl.semaphore_signal(
                barrier, inc=1, device_id={"space": lax.rem(me + k, self.n)}, device_id_type=MESH
            )
        if chan:
            pl.semaphore_signal(
                barrier, inc=1, device_id={"chan": 1 - lax.axis_index("chan")}, device_id_type=MESH
            )
        pl.semaphore_wait(barrier, self.n - 1 + (1 if chan else 0))

    def source(self, x, d):
        return x.at[:, d] if self.spread else x.at[pl.ds(d * self.held, self.held)]

    def slot(self, y, s):
        return y.at[pl.ds(s * self.held, self.held)] if self.spread else y.at[:, s]

    def when(self, other, run):
        if self.sparse:
            pl.when(lax.axis_index("space") + other >= self.n - 1)(run)
        else:
            run()

    def copy(self, x, y, k, send_sem, recv_sem, sending):
        me = lax.axis_index("space")
        other = lax.rem(me + k, self.n) if sending else lax.rem(me + self.n - k, self.n)
        return other, pltpu.make_async_remote_copy(
            src_ref=self.source(x, other),
            dst_ref=self.slot(y, me if sending else other),
            send_sem=send_sem.at[k],
            recv_sem=recv_sem.at[k],
            device_id={"space": other},
            device_id_type=MESH,
        )


def send_all(ex, x, y, send_sem, recv_sem):
    for k in range(1, ex.n):
        other, copy = ex.copy(x, y, k, send_sem, recv_sem, True)
        ex.when(other, copy.start)


def wait_sends(ex, x, y, send_sem, recv_sem):
    for k in range(1, ex.n):
        other, copy = ex.copy(x, y, k, send_sem, recv_sem, True)
        ex.when(other, copy.wait_send)


def zero_fill(ex, targets, zero, zero_sem, start):
    me = lax.axis_index("space")
    for k in range(ex.n):
        other = lax.rem(me + ex.n - k, ex.n)

        @pl.when(me + other < ex.n - 1)
        def _():
            for i, y in enumerate(targets):
                copy = pltpu.make_async_copy(zero, ex.slot(y, other), zero_sem.at[i, k])
                copy.start() if start else copy.wait()


def plain_kernel(ex, legendre, *refs):
    if legendre is not None:
        x, log_start, rows, y, analysis, synthesis, values = refs[:7]
        send_sem, recv_sem, own_sem = refs[7:]
    elif ex.sparse:
        x, y, zero, zero_sem, send_sem, recv_sem, own_sem = refs
    else:
        x, y, send_sem, recv_sem, own_sem = refs
    me = lax.axis_index("space")
    ex.greet(False)
    send_all(ex, x, y, send_sem, recv_sem)
    own = pltpu.make_async_copy(ex.source(x, me), ex.slot(y, me), own_sem)
    ex.when(me, own.start)
    if ex.sparse:
        zero[...] = jnp.zeros_like(zero)
        zero_fill(ex, [y], zero, zero_sem, True)
    if legendre is not None:
        first_order = (ex.n - 1 - me) * ex.held
        legendre_into(log_start, rows, legendre, first_order, values, analysis, synthesis)
    ex.when(me, own.wait)
    for k in range(1, ex.n):
        other, copy = ex.copy(x, y, k, send_sem, recv_sem, False)
        ex.when(other, copy.wait_recv)
    wait_sends(ex, x, y, send_sem, recv_sem)
    if ex.sparse:
        zero_fill(ex, [y], zero, zero_sem, False)


def gather_kernel(ex, by_channel, x, y, zero, zero_sem, send_sem, recv_sem, own_sem, fsend, frecv):
    me = lax.axis_index("space")
    chan = lax.axis_index("chan")
    mine = y.at[chan] if by_channel else y.at[0]
    theirs = y.at[chan] if by_channel else y.at[1]
    coming = y.at[1 - chan] if by_channel else y.at[1]
    ex.greet(True)
    send_all(ex, x, mine, send_sem, recv_sem)

    def forward(k, other, source):
        return pltpu.make_async_remote_copy(
            src_ref=source,
            dst_ref=ex.slot(theirs, other),
            send_sem=fsend.at[k],
            recv_sem=frecv.at[k],
            device_id={"chan": 1 - chan},
            device_id_type=MESH,
        )

    own = pltpu.make_async_copy(ex.source(x, me), ex.slot(mine, me), own_sem)
    ex.when(me, own.start)
    ex.when(me, forward(0, me, ex.source(x, me)).start)
    zero[...] = jnp.zeros_like(zero)
    zero_fill(ex, [y.at[0], y.at[1]], zero, zero_sem, True)
    for k in range(1, ex.n):
        other, copy = ex.copy(x, mine, k, send_sem, recv_sem, False)

        def pass_on(copy=copy, k=k, other=other):
            copy.wait_recv()
            forward(k, other, ex.slot(mine, other)).start()

        ex.when(other, pass_on)
    ex.when(me, own.wait)
    for k in range(ex.n):
        other = lax.rem(me + ex.n - k, ex.n)

        def settle(k=k, other=other):
            copy = pltpu.make_async_remote_copy(
                src_ref=ex.slot(mine, other),
                dst_ref=ex.slot(coming, other),
                send_sem=fsend.at[k],
                recv_sem=frecv.at[k],
                device_id={"chan": 1 - chan},
                device_id_type=MESH,
            )
            copy.wait_recv()
            copy.wait_send()

        ex.when(other, settle)
    wait_sends(ex, x, mine, send_sem, recv_sem)
    zero_fill(ex, [y.at[0], y.at[1]], zero, zero_sem, False)


def any_spec():
    return pl.BlockSpec(memory_space=pl.ANY)


def vmem_spec():
    return pl.BlockSpec(memory_space=pltpu.VMEM)


def params(collective_id):
    return pltpu.CompilerParams(
        collective_id=collective_id, has_side_effects=True, vmem_limit_bytes=24 * 2**20
    )


def swap(x, n, spread, sparse, collective_id, legendre=None):
    if spread:
        held, _, rows, width = x.shape
        shape = (n * held, rows, width)
    else:
        total, rows, width = x.shape
        held = total // n
        shape = (held, n, rows, width)
    ex = Exchange(n, held, spread, sparse)
    sems = [
        pltpu.SemaphoreType.DMA((n,)),
        pltpu.SemaphoreType.DMA((n,)),
        pltpu.SemaphoreType.DMA,
    ]
    out = jax.ShapeDtypeStruct(shape, x.dtype)
    if legendre is not None:
        log_start, rows_in, scale = legendre
        orders, latitudes = log_start.shape
        table = jax.ShapeDtypeStruct((orders, n * held, latitudes), jnp.bfloat16)
        return pl.pallas_call(
            functools.partial(plain_kernel, ex, scale),
            out_shape=(out, table, table),
            in_specs=[any_spec(), vmem_spec(), vmem_spec()],
            out_specs=(any_spec(), vmem_spec(), vmem_spec()),
            scratch_shapes=[pltpu.VMEM((orders, n * held, latitudes), jnp.float32)] + sems,
            compiler_params=params(collective_id),
            name="exchange_and_legendre",
        )(x, log_start, rows_in)
    scratch = list(sems)
    if sparse:
        zeros = [pltpu.VMEM((held, rows, width), x.dtype), pltpu.SemaphoreType.DMA((1, n))]
        scratch = zeros + scratch
    return pl.pallas_call(
        functools.partial(plain_kernel, ex, None),
        out_shape=out,
        in_specs=[any_spec()],
        out_specs=any_spec(),
        scratch_shapes=scratch,
        compiler_params=params(collective_id),
        name="exchange",
    )(x)


def swap_gather(x, n, by_channel, collective_id):
    total, rows, width = x.shape
    held = total // n
    ex = Exchange(n, held, False, True)
    return pl.pallas_call(
        functools.partial(gather_kernel, ex, by_channel),
        out_shape=jax.ShapeDtypeStruct((2, held, n, rows, width), x.dtype),
        in_specs=[any_spec()],
        out_specs=any_spec(),
        scratch_shapes=[
            pltpu.VMEM((held, rows, width), x.dtype),
            pltpu.SemaphoreType.DMA((2, n)),
            pltpu.SemaphoreType.DMA((n,)),
            pltpu.SemaphoreType.DMA((n,)),
            pltpu.SemaphoreType.DMA,
            pltpu.SemaphoreType.DMA((n,)),
            pltpu.SemaphoreType.DMA((n,)),
        ],
        compiler_params=params(collective_id),
        name="exchange_and_gather",
    )(x)


def flat(block):
    rows = block.shape[0] * block.shape[1]
    return block.astype(jnp.float32).reshape(rows, block.shape[2]).astype(block.dtype)


def unflat(values, n):
    return values.reshape(n, values.shape[0] // n, values.shape[1]).astype(jnp.bfloat16)


def mm(left, right):
    return jnp.dot(left, right, preferred_element_type=jnp.float32)


CHUNK = 4


class Chunked:
    def __init__(self, n, held):
        self.n, self.held = n, held
        self.chunks = held // CHUNK

    def band(self, f, c, d):
        return f.at[pl.ds(c * CHUNK, CHUNK), d]

    def lats(self, y, c, s):
        return y.at[pl.ds(s * self.held + c * CHUNK, CHUNK)]

    def copy(self, x, y, c, k, send_sem, recv_sem, sending, outward):
        me = lax.axis_index("space")
        other = lax.rem(me + k, self.n) if sending else lax.rem(me + self.n - k, self.n)
        here = me if sending else other
        if outward:
            src, dst = self.band(x, c, other), self.lats(y, c, here)
        else:
            src, dst = self.lats(x, c, other), self.band(y, c, here)
        return pltpu.make_async_remote_copy(
            src_ref=src,
            dst_ref=dst,
            send_sem=send_sem.at[c, k],
            recv_sem=recv_sem.at[c, k],
            device_id={"space": other},
            device_id_type=MESH,
        )

    def own(self, x, y, c, sem, outward):
        me = lax.axis_index("space")
        if outward:
            return pltpu.make_async_copy(self.band(x, c, me), self.lats(y, c, me), sem.at[c])
        return pltpu.make_async_copy(self.lats(x, c, me), self.band(y, c, me), sem.at[c])


def fourier_kernel(
    ex,
    synthesis_scale,
    field,
    weight,
    forward,
    log_start,
    rows,
    y,
    analysis,
    synthesis,
    weights,
    values,
    held_field,
    bands,
    load_sem,
    send_sem,
    recv_sem,
    own_sem,
    weight_sem,
):
    n, ch = ex.n, Chunked(ex.n, ex.held)
    me = lax.axis_index("space")
    chan = lax.axis_index("chan")
    half = weight.shape[2]
    loads = [
        pltpu.make_async_copy(
            field.at[pl.ds(c * CHUNK, CHUNK)], held_field.at[pl.ds(c * CHUNK, CHUNK)], load_sem.at[c]
        )
        for c in range(ch.chunks)
    ]
    for load in loads:
        load.start()
    ex.greet(True)
    keep = pltpu.make_async_copy(
        weight.at[:, pl.ds(pl.multiple_of(chan * half, half), half)], weights.at[0], weight_sem.at[0]
    )
    give = pltpu.make_async_remote_copy(
        src_ref=weight.at[:, pl.ds(pl.multiple_of((1 - chan) * half, half), half)],
        dst_ref=weights.at[1],
        send_sem=weight_sem.at[1],
        recv_sem=weight_sem.at[2],
        device_id={"chan": 1 - chan},
        device_id_type=MESH,
    )
    for c in range(ch.chunks):
        loads[c].wait()

        def pair(i, carry, c=c):
            j = c * CHUNK + 2 * i
            wide = jnp.concatenate([held_field[j], held_field[j + 1]], axis=1)
            out = mm(forward[...], wide)
            bands[j] = unflat(out[:, :half], n)
            bands[j + 1] = unflat(out[:, half:], n)
            return carry

        lax.fori_loop(0, CHUNK // 2, pair, 0)
        for k in range(1, n):
            ch.copy(bands, y, c, k, send_sem, recv_sem, True, True).start()
        ch.own(bands, y, c, own_sem, True).start()
    keep.start()
    give.start()
    first_order = (n - 1 - me) * ex.held
    legendre_into(log_start, rows, synthesis_scale, first_order, values, analysis, synthesis)
    for c in range(ch.chunks):
        ch.own(bands, y, c, own_sem, True).wait()
        for k in range(1, n):
            ch.copy(bands, y, c, k, send_sem, recv_sem, False, True).wait_recv()
            ch.copy(bands, y, c, k, send_sem, recv_sem, True, True).wait_send()
    keep.wait()
    give.wait()


def fourier_exchange(field, weight, forward, n, rows, log_start, rows_in, scale, collective_id):
    held, longitudes, half = field.shape
    orders, latitudes = log_start.shape
    degrees = weight.shape[0]
    ex = Exchange(n, held, True, False)
    chunks = held // CHUNK
    table = jax.ShapeDtypeStruct((orders, degrees * n, latitudes), jnp.bfloat16)
    return pl.pallas_call(
        functools.partial(fourier_kernel, ex, scale),
        out_shape=(
            jax.ShapeDtypeStruct((n * held, rows, half), field.dtype),
            table,
            table,
            jax.ShapeDtypeStruct((2, degrees, half, half), field.dtype),
        ),
        in_specs=[any_spec(), any_spec(), vmem_spec(), vmem_spec(), vmem_spec()],
        out_specs=(any_spec(), vmem_spec(), vmem_spec(), any_spec()),
        scratch_shapes=[
            pltpu.VMEM((orders, degrees * n, latitudes), jnp.float32),
            pltpu.VMEM((held, longitudes, half), field.dtype),
            pltpu.VMEM((held, n, rows, half), field.dtype),
            pltpu.SemaphoreType.DMA((chunks,)),
            pltpu.SemaphoreType.DMA((chunks, n)),
            pltpu.SemaphoreType.DMA((chunks, n)),
            pltpu.SemaphoreType.DMA((chunks,)),
            pltpu.SemaphoreType.DMA((3,)),
        ],
        compiler_params=params(collective_id),
        name="fourier_exchange",
    )(field, weight, forward, log_start, rows_in)


TILE = 128


def response_kernel(
    ex,
    grid,
    field,
    cotangent,
    inverse_t,
    inverse,
    output,
    y,
    held_field,
    held_cot,
    arrived,
    slopes,
    bands,
    load_sem,
    in_send,
    in_recv,
    in_own,
    out_send,
    out_recv,
    out_own,
    store_sem,
):
    n, ch = ex.n, Chunked(ex.n, ex.held)
    half = field.shape[2]
    tiles = field.shape[1] // TILE

    def part(ref, c):
        return ref.at[pl.ds(c * CHUNK, CHUNK)]

    def loads(c):
        return (
            pltpu.make_async_copy(part(field, c), part(held_field, c), load_sem.at[0, c]),
            pltpu.make_async_copy(part(cotangent, c), part(held_cot, c), load_sem.at[1, c]),
        )

    def store(c):
        return pltpu.make_async_copy(part(held_field, c), part(output, c), store_sem.at[c])

    for c in range(ch.chunks):
        for load in loads(c):
            load.start()
    ex.greet(False)
    for c in range(ch.chunks):
        for k in range(1, n):
            ch.copy(grid, arrived, c, k, in_send, in_recv, True, False).start()
        ch.own(grid, arrived, c, in_own, False).start()
    for c in range(ch.chunks):
        for load in loads(c):
            load.wait()
        ch.own(grid, arrived, c, in_own, False).wait()
        for k in range(1, n):
            ch.copy(grid, arrived, c, k, in_send, in_recv, False, False).wait_recv()

        def pair(i, carry, c=c):
            j = c * CHUNK + 2 * i
            wide = jnp.concatenate([flat(arrived[j]), flat(arrived[j + 1])], axis=1)

            def tile(t, inner):
                at = pl.ds(pl.multiple_of(t * TILE, TILE), TILE)
                response = mm(inverse_t[at, :], wide)
                cdf = 0.5 * (1.0 + lax.erf(response * (1.0 / math.sqrt(2.0))))
                density = jnp.exp(-0.5 * response * response) * (1.0 / math.sqrt(2.0 * math.pi))
                gain = response * cdf
                slope = cdf + response * density
                for side in range(2):
                    lanes = slice(side * half, (side + 1) * half)
                    base = held_field[j + side, at, :].astype(jnp.float32)
                    held_field[j + side, at, :] = (base + gain[:, lanes]).astype(jnp.bfloat16)
                    cot = held_cot[j + side, at, :].astype(jnp.float32)
                    slopes[at, lanes] = (cot * slope[:, lanes]).astype(jnp.bfloat16)
                return inner

            lax.fori_loop(0, tiles, tile, 0)
            out = mm(inverse[...], slopes[...])
            bands[j] = unflat(out[:, :half], n)
            bands[j + 1] = unflat(out[:, half:], n)
            return carry

        lax.fori_loop(0, CHUNK // 2, pair, 0)
        for k in range(1, n):
            ch.copy(bands, y, c, k, out_send, out_recv, True, True).start()
        ch.own(bands, y, c, out_own, True).start()
        store(c).start()
    for c in range(ch.chunks):
        ch.own(bands, y, c, out_own, True).wait()
        store(c).wait()
        for k in range(1, n):
            ch.copy(bands, y, c, k, out_send, out_recv, False, True).wait_recv()
            ch.copy(bands, y, c, k, out_send, out_recv, True, True).wait_send()
            ch.copy(grid, arrived, c, k, in_send, in_recv, True, False).wait_send()


def response_exchange(grid, field, cotangent, inverse_t, inverse, n, collective_id):
    held, longitudes, half = field.shape
    rows = grid.shape[1]
    chunks = held // CHUNK
    ex = Exchange(n, held, True, False)
    return pl.pallas_call(
        functools.partial(response_kernel, ex),
        out_shape=(
            jax.ShapeDtypeStruct(field.shape, field.dtype),
            jax.ShapeDtypeStruct((n * held, rows, half), field.dtype),
        ),
        in_specs=[any_spec()] * 3 + [vmem_spec()] * 2,
        out_specs=(any_spec(), any_spec()),
        scratch_shapes=[
            pltpu.VMEM((held, longitudes, half), field.dtype),
            pltpu.VMEM((held, longitudes, half), field.dtype),
            pltpu.VMEM((held, n, rows, half), field.dtype),
            pltpu.VMEM((longitudes, 2 * half), field.dtype),
            pltpu.VMEM((held, n, rows, half), field.dtype),
            pltpu.SemaphoreType.DMA((2, chunks)),
            pltpu.SemaphoreType.DMA((chunks, n)),
            pltpu.SemaphoreType.DMA((chunks, n)),
            pltpu.SemaphoreType.DMA((chunks,)),
            pltpu.SemaphoreType.DMA((chunks, n)),
            pltpu.SemaphoreType.DMA((chunks, n)),
            pltpu.SemaphoreType.DMA((chunks,)),
            pltpu.SemaphoreType.DMA((chunks,)),
        ],
        compiler_params=params(collective_id),
        name="response_exchange",
    )(grid, field, cotangent, inverse_t, inverse)


def field_grad_kernel(band, cotangent, forward_t, out):
    half = band.shape[-1]
    for i in range(0, band.shape[0], 2):
        wide = jnp.concatenate([flat(band[i]), flat(band[i + 1])], axis=1)
        total = mm(forward_t[...], wide)
        for side in range(2):
            part = total[:, side * half : (side + 1) * half]
            out[i + side] = (cotangent[i + side].astype(jnp.float32) + part).astype(out.dtype)


def final_field_grad(band, cotangent, forward_t):
    held, n, rows, half = band.shape
    longitudes = cotangent.shape[1]
    lat = pl.BlockSpec((2, longitudes, half), lambda i: (i, 0, 0))
    return pl.pallas_call(
        field_grad_kernel,
        grid=(held // 2,),
        out_shape=jax.ShapeDtypeStruct(cotangent.shape, cotangent.dtype),
        in_specs=[
            pl.BlockSpec((2, n, rows, half), lambda i: (i, 0, 0, 0)),
            lat,
            pl.BlockSpec(forward_t.shape, lambda i: (0, 0)),
        ],
        out_specs=lat,
        compiler_params=pltpu.CompilerParams(vmem_limit_bytes=24 * 2**20),
        name="field_grad",
    )(band, cotangent, forward_t)


def mix_back_kernel(
    ex, scale, coeffs, grads, weights, y, weight_grad, mixed, zero, zero_sem, send_sem, recv_sem, own_sem
):
    n = ex.n
    me = lax.axis_index("space")
    half = weights.shape[-1]
    ex.greet(False)
    turned = (((1,), (1,)), ((), ()))

    def degree(at, carry):
        total = lax.dot_general(
            flat(grads[0, at]), weights[0, at], turned, preferred_element_type=jnp.float32
        ) + lax.dot_general(
            flat(grads[1, at]), weights[1, at], turned, preferred_element_type=jnp.float32
        )
        mixed[at] = unflat(total * scale, n)
        return carry

    lax.fori_loop(0, ex.held, degree, 0)
    send_all(ex, mixed, y, send_sem, recv_sem)
    own = pltpu.make_async_copy(ex.source(mixed, me), ex.slot(y, me), own_sem)
    ex.when(me, own.start)
    zero[...] = jnp.zeros_like(zero)
    zero_fill(ex, [y], zero, zero_sem, True)
    summed = (((0,), (0,)), ((), ()))

    def products(at, carry):
        grad = flat(grads[0, at])
        for side in range(2):
            part = lax.dot_general(
                flat(coeffs[side, at]), grad, summed, preferred_element_type=jnp.float32
            )
            weight_grad[at, pl.ds(side * half, half), :] = (part * scale).astype(jnp.bfloat16)
        return carry

    lax.fori_loop(0, ex.held, products, 0)
    ex.when(me, own.wait)
    for k in range(1, n):
        other, copy = ex.copy(mixed, y, k, send_sem, recv_sem, False)
        ex.when(other, copy.wait_recv)
    wait_sends(ex, mixed, y, send_sem, recv_sem)
    zero_fill(ex, [y], zero, zero_sem, False)


def mix_back(coeffs, grads, weights, scale, collective_id):
    _, held, n, rows, half = coeffs.shape
    ex = Exchange(n, held, True, True)
    return pl.pallas_call(
        functools.partial(mix_back_kernel, ex, scale),
        out_shape=(
            jax.ShapeDtypeStruct((n * held, rows, half), coeffs.dtype),
            jax.ShapeDtypeStruct((held, 2 * half, half), coeffs.dtype),
        ),
        in_specs=[vmem_spec()] * 3,
        out_specs=(any_spec(), vmem_spec()),
        scratch_shapes=[
            pltpu.VMEM((held, n, rows, half), coeffs.dtype),
            pltpu.VMEM((held, rows, half), coeffs.dtype),
            pltpu.SemaphoreType.DMA((1, n)),
            pltpu.SemaphoreType.DMA((n,)),
            pltpu.SemaphoreType.DMA((n,)),
            pltpu.SemaphoreType.DMA,
        ],
        compiler_params=params(collective_id),
        name="mix_back",
    )(coeffs, grads, weights)


def dot32(formula, left, right):
    return jnp.einsum(formula, left, right, preferred_element_type=jnp.float32)


def local(field, spectral_weight, cotangent):
    n = lax.axis_size("space")
    held, longitudes, half = field.shape
    degrees_held, channels, _ = spectral_weight.shape
    latitudes = held * n
    degrees = degrees_held * n
    orders_held = degrees_held
    rows = 2 * orders_held
    mix_scale = 1.0 / math.sqrt(channels)
    chan = lax.axis_index("chan")
    block = n - 1 - lax.axis_index("space")
    order_list = np.arange(degrees).reshape(n, orders_held)[::-1].reshape(-1)
    forward_np, inverse_np = fourier_tables(longitudes, order_list)
    forward, inverse = jnp.asarray(forward_np), jnp.asarray(inverse_np)
    log_np, rows_np, scale = latitude_rows(latitudes, longitudes, degrees)
    log_start = lax.dynamic_slice_in_dim(jnp.asarray(log_np), block * orders_held, orders_held, 0)

    weight_halves = spectral_weight.reshape(degrees_held, 2, half, half)
    by_order, analysis, synthesis, weights = fourier_exchange(
        field, spectral_weight, forward, n, rows, log_start, jnp.asarray(rows_np), scale, 0
    )

    def to_degrees(table, values):
        values = values.reshape(latitudes, orders_held, 2, half)
        out = dot32("mlj,jmrc->lmrc", table, values).astype(jnp.bfloat16)
        return out.reshape(degrees, rows, half)

    def to_latitudes(table, values):
        values = values.reshape(degrees, orders_held, 2, half)
        out = dot32("mlj,lmrc->jmrc", table, values).astype(jnp.bfloat16)
        return out.reshape(latitudes, rows, half)

    blocks = swap_gather(to_degrees(analysis, by_order), n, True, 1)
    coeffs = blocks.reshape(2, degrees_held, n * rows, half)
    mixed = (
        dot32("lqc,lco->lqo", coeffs[0], weight_halves[:, 0])
        + dot32("lqc,lco->lqo", coeffs[1], weight_halves[:, 1])
    ) * mix_scale
    mixed = mixed.astype(jnp.bfloat16).reshape(degrees_held, n, rows, half)
    mixed_orders = swap(mixed, n, True, True, 2)
    output, grad_by_order = response_exchange(
        to_latitudes(synthesis, mixed_orders),
        field,
        cotangent,
        jnp.asarray(np.ascontiguousarray(inverse_np.T)),
        inverse,
        n,
        3,
    )
    grads = swap_gather(to_degrees(synthesis, grad_by_order), n, False, 5)
    coeff_orders, weight_grad = mix_back(blocks, grads, weights, mix_scale, 6)
    fourier_band = swap(to_latitudes(analysis, coeff_orders), n, False, False, 7)
    field_grad = final_field_grad(
        fourier_band, cotangent, jnp.asarray(np.ascontiguousarray(forward_np.T))
    )
    return (output, field_grad, weight_grad)


def solution(mesh):
    in_specs = (
        P(("parts", "space"), None, "chan"),
        P("space", None, "chan"),
        P(("parts", "space"), None, "chan"),
    )
    out_specs = (
        P(("parts", "space"), None, "chan"),
        P(("parts", "space"), None, "chan"),
        P(("parts", "space"), None, "chan"),
    )
    return jax.shard_map(local, mesh=mesh, in_specs=in_specs, out_specs=out_specs, check_vma=False)
```

```python
import functools
import math

import jax
import jax.numpy as jnp
import ml_dtypes
import numpy as np
from jax import lax
from jax.experimental import pallas as pl
from jax.experimental.pallas import tpu as pltpu
from jax.sharding import PartitionSpec as P

LIMIT = 2.0**40
SHRINK = 2.0 ** (-40)
LOGSTEP = 40.0 * math.log(2.0)
MESH = pl.DeviceIdType.MESH


def fourier_tables(longitudes, order_list):
    products = (np.asarray(order_list)[:, None] * np.arange(longitudes)[None, :]) % longitudes
    angle = 2.0 * math.pi / longitudes * products
    table = np.stack([np.cos(angle), -np.sin(angle)], axis=1)
    weights = np.where(np.asarray(order_list) == 0, 1.0, 2.0)[:, None, None]
    forward = table.reshape(-1, longitudes).astype(np.float32)
    inverse = (table * weights).reshape(-1, longitudes).astype(np.float32)
    return forward.astype(ml_dtypes.bfloat16), inverse.astype(ml_dtypes.bfloat16)


def latitude_rows(latitudes, longitudes, orders):
    half = latitudes // 2
    north = (np.arange(half) + 0.5) * (math.pi / latitudes)
    cosines = np.concatenate([np.cos(north), -np.cos(north)[::-1]])
    sines = np.concatenate([np.sin(north), np.sin(north)[::-1]])
    order = np.arange(orders)
    gammas = np.array([math.lgamma(m + 0.5) - math.lgamma(m + 1.0) for m in order])
    start = 0.5 * (np.log((2.0 * order + 1.0) / (4.0 * math.pi)) + gammas - 0.5 * math.log(math.pi))
    log_start = start[:, None] + order[:, None] * np.log(sines)[None, :]
    area = latitudes * longitudes
    rows = np.stack([cosines, math.pi**1.5 / math.sqrt(area) * sines])
    return (
        log_start.astype(np.float32),
        rows.astype(np.float32),
        math.sqrt(4.0 * math.pi / area),
    )


def legendre_into(log_start, rows, synthesis_scale, first_order, values, analysis, synthesis):
    held, degrees, latitudes = values.shape
    shape = (held, latitudes)
    order = (lax.broadcasted_iota(jnp.int32, shape, 0) + first_order).astype(jnp.float32)
    cosines = jnp.broadcast_to(rows[0:1, :], shape)
    start = log_start[...]

    def step(at, state):
        previous, before, rescales = state
        degree = at.astype(jnp.float32)
        lower_deg = degree - 1.0
        square = order * order
        upper = jnp.sqrt((4.0 * degree * degree - 1.0) / jnp.maximum(degree * degree - square, 1.0))
        lower = jnp.sqrt(
            jnp.maximum(lower_deg * lower_deg - square, 0.0)
            / jnp.maximum(4.0 * lower_deg * lower_deg - 1.0, 1.0)
        )
        newest = jnp.where(
            degree == order,
            1.0,
            jnp.where(degree > order, upper * (cosines * previous - lower * before), 0.0),
        )
        too_large = jnp.abs(newest) > LIMIT
        newest = jnp.where(too_large, newest * SHRINK, newest)
        previous = jnp.where(too_large, previous * SHRINK, previous)
        rescales = rescales + jnp.where(too_large, 1.0, 0.0)
        values[:, pl.ds(at, 1), :] = (newest * jnp.exp(start + rescales * LOGSTEP))[:, None, :]
        return newest, previous, rescales

    zero = jnp.zeros(shape, jnp.float32)
    lax.fori_loop(0, degrees, step, (zero, zero, zero))
    quadrature = rows[1:2, :]

    def finish(m, carry):
        analysis[m] = (values[m] * quadrature).astype(jnp.bfloat16)
        synthesis[m] = (values[m] * synthesis_scale).astype(jnp.bfloat16)
        return carry

    lax.fori_loop(0, held, finish, 0)


class Exchange:
    def __init__(self, n, held, spread, sparse):
        self.n, self.held, self.spread, self.sparse = n, held, spread, sparse

    def greet(self, chan):
        me = lax.axis_index("space")
        barrier = pltpu.get_barrier_semaphore()
        for k in range(1, self.n):
            pl.semaphore_signal(
                barrier, inc=1, device_id={"space": lax.rem(me + k, self.n)}, device_id_type=MESH
            )
        if chan:
            pl.semaphore_signal(
                barrier, inc=1, device_id={"chan": 1 - lax.axis_index("chan")}, device_id_type=MESH
            )
        pl.semaphore_wait(barrier, self.n - 1 + (1 if chan else 0))

    def source(self, x, d):
        return x.at[:, d] if self.spread else x.at[pl.ds(d * self.held, self.held)]

    def slot(self, y, s):
        return y.at[pl.ds(s * self.held, self.held)] if self.spread else y.at[:, s]

    def when(self, other, run):
        if self.sparse:
            pl.when(lax.axis_index("space") + other >= self.n - 1)(run)
        else:
            run()

    def copy(self, x, y, k, send_sem, recv_sem, sending):
        me = lax.axis_index("space")
        other = lax.rem(me + k, self.n) if sending else lax.rem(me + self.n - k, self.n)
        return other, pltpu.make_async_remote_copy(
            src_ref=self.source(x, other),
            dst_ref=self.slot(y, me if sending else other),
            send_sem=send_sem.at[k],
            recv_sem=recv_sem.at[k],
            device_id={"space": other},
            device_id_type=MESH,
        )


def send_all(ex, x, y, send_sem, recv_sem):
    for k in range(1, ex.n):
        other, copy = ex.copy(x, y, k, send_sem, recv_sem, True)
        ex.when(other, copy.start)


def wait_sends(ex, x, y, send_sem, recv_sem):
    for k in range(1, ex.n):
        other, copy = ex.copy(x, y, k, send_sem, recv_sem, True)
        ex.when(other, copy.wait_send)


def zero_fill(ex, targets, zero, zero_sem, start):
    me = lax.axis_index("space")
    for k in range(ex.n):
        other = lax.rem(me + ex.n - k, ex.n)

        @pl.when(me + other < ex.n - 1)
        def _():
            for i, y in enumerate(targets):
                copy = pltpu.make_async_copy(zero, ex.slot(y, other), zero_sem.at[i, k])
                copy.start() if start else copy.wait()


def plain_kernel(ex, legendre, *refs):
    if legendre is not None:
        x, log_start, rows, y, analysis, synthesis, values = refs[:7]
        send_sem, recv_sem, own_sem = refs[7:]
    elif ex.sparse:
        x, y, zero, zero_sem, send_sem, recv_sem, own_sem = refs
    else:
        x, y, send_sem, recv_sem, own_sem = refs
    me = lax.axis_index("space")
    ex.greet(False)
    send_all(ex, x, y, send_sem, recv_sem)
    own = pltpu.make_async_copy(ex.source(x, me), ex.slot(y, me), own_sem)
    ex.when(me, own.start)
    if ex.sparse:
        zero[...] = jnp.zeros_like(zero)
        zero_fill(ex, [y], zero, zero_sem, True)
    if legendre is not None:
        first_order = (ex.n - 1 - me) * ex.held
        legendre_into(log_start, rows, legendre, first_order, values, analysis, synthesis)
    ex.when(me, own.wait)
    for k in range(1, ex.n):
        other, copy = ex.copy(x, y, k, send_sem, recv_sem, False)
        ex.when(other, copy.wait_recv)
    wait_sends(ex, x, y, send_sem, recv_sem)
    if ex.sparse:
        zero_fill(ex, [y], zero, zero_sem, False)


def any_spec():
    return pl.BlockSpec(memory_space=pl.ANY)


def hbm_spec():
    return pl.BlockSpec(memory_space=pltpu.HBM)


def vmem_spec():
    return pl.BlockSpec(memory_space=pltpu.VMEM)


def params(collective_id):
    return pltpu.CompilerParams(
        collective_id=collective_id, has_side_effects=True, vmem_limit_bytes=24 * 2**20
    )


def swap(x, n, spread, sparse, collective_id, legendre=None):
    if spread:
        held, _, rows, width = x.shape
        shape = (n * held, rows, width)
    else:
        total, rows, width = x.shape
        held = total // n
        shape = (held, n, rows, width)
    ex = Exchange(n, held, spread, sparse)
    sems = [
        pltpu.SemaphoreType.DMA((n,)),
        pltpu.SemaphoreType.DMA((n,)),
        pltpu.SemaphoreType.DMA,
    ]
    out = jax.ShapeDtypeStruct(shape, x.dtype)
    if legendre is not None:
        log_start, rows_in, scale = legendre
        orders, latitudes = log_start.shape
        table = jax.ShapeDtypeStruct((orders, n * held, latitudes), jnp.bfloat16)
        return pl.pallas_call(
            functools.partial(plain_kernel, ex, scale),
            out_shape=(out, table, table),
            in_specs=[any_spec(), vmem_spec(), vmem_spec()],
            out_specs=(any_spec(), vmem_spec(), vmem_spec()),
            scratch_shapes=[pltpu.VMEM((orders, n * held, latitudes), jnp.float32)] + sems,
            compiler_params=params(collective_id),
            name="exchange_and_legendre",
        )(x, log_start, rows_in)
    scratch = list(sems)
    if sparse:
        zeros = [pltpu.VMEM((held, rows, width), x.dtype), pltpu.SemaphoreType.DMA((1, n))]
        scratch = zeros + scratch
    return pl.pallas_call(
        functools.partial(plain_kernel, ex, None),
        out_shape=out,
        in_specs=[any_spec()],
        out_specs=any_spec(),
        scratch_shapes=scratch,
        compiler_params=params(collective_id),
        name="exchange",
    )(x)


def flat(block):
    rows = block.shape[0] * block.shape[1]
    return block.astype(jnp.float32).reshape(rows, block.shape[2]).astype(block.dtype)


def unflat(values, n):
    return values.reshape(n, values.shape[0] // n, values.shape[1]).astype(jnp.bfloat16)


def mm(left, right):
    return jnp.dot(left, right, preferred_element_type=jnp.float32)


CHUNK = 4


class Chunked:
    def __init__(self, n, held):
        self.n, self.held = n, held
        self.chunks = held // CHUNK

    def band(self, f, c, d):
        return f.at[pl.ds(c * CHUNK, CHUNK), d]

    def lats(self, y, c, s):
        return y.at[pl.ds(s * self.held + c * CHUNK, CHUNK)]

    def copy(self, x, y, c, k, send_sem, recv_sem, sending, outward):
        me = lax.axis_index("space")
        other = lax.rem(me + k, self.n) if sending else lax.rem(me + self.n - k, self.n)
        here = me if sending else other
        if outward:
            src, dst = self.band(x, c, other), self.lats(y, c, here)
        else:
            src, dst = self.lats(x, c, other), self.band(y, c, here)
        return pltpu.make_async_remote_copy(
            src_ref=src,
            dst_ref=dst,
            send_sem=send_sem.at[c, k],
            recv_sem=recv_sem.at[c, k],
            device_id={"space": other},
            device_id_type=MESH,
        )

    def own(self, x, y, c, sem, outward):
        me = lax.axis_index("space")
        if outward:
            return pltpu.make_async_copy(self.band(x, c, me), self.lats(y, c, me), sem.at[c])
        return pltpu.make_async_copy(self.lats(x, c, me), self.band(y, c, me), sem.at[c])


def fourier_kernel(
    ex,
    synthesis_scale,
    field,
    weight,
    forward,
    log_start,
    rows,
    y,
    analysis,
    synthesis,
    weights,
    values,
    held_field,
    bands,
    load_sem,
    send_sem,
    recv_sem,
    own_sem,
    weight_sem,
):
    n, ch = ex.n, Chunked(ex.n, ex.held)
    me = lax.axis_index("space")
    chan = lax.axis_index("chan")
    half = weight.shape[2]
    loads = [
        pltpu.make_async_copy(
            field.at[pl.ds(c * CHUNK, CHUNK)], held_field.at[pl.ds(c * CHUNK, CHUNK)], load_sem.at[c]
        )
        for c in range(ch.chunks)
    ]
    for load in loads:
        load.start()
    ex.greet(True)
    keep = pltpu.make_async_copy(
        weight.at[:, pl.ds(pl.multiple_of(chan * half, half), half)], weights.at[0], weight_sem.at[0]
    )
    give = pltpu.make_async_remote_copy(
        src_ref=weight.at[:, pl.ds(pl.multiple_of((1 - chan) * half, half), half)],
        dst_ref=weights.at[1],
        send_sem=weight_sem.at[1],
        recv_sem=weight_sem.at[2],
        device_id={"chan": 1 - chan},
        device_id_type=MESH,
    )
    for c in range(ch.chunks):
        loads[c].wait()

        def pair(i, carry, c=c):
            j = c * CHUNK + 2 * i
            wide = jnp.concatenate([held_field[j], held_field[j + 1]], axis=1)
            out = mm(forward[...], wide)
            bands[j] = unflat(out[:, :half], n)
            bands[j + 1] = unflat(out[:, half:], n)
            return carry

        lax.fori_loop(0, CHUNK // 2, pair, 0)
        for k in range(1, n):
            ch.copy(bands, y, c, k, send_sem, recv_sem, True, True).start()
        ch.own(bands, y, c, own_sem, True).start()
    keep.start()
    give.start()
    first_order = (n - 1 - order_block(me)) * analysis.shape[0]
    legendre_into(log_start, rows, synthesis_scale, first_order, values, analysis, synthesis)
    for c in range(ch.chunks):
        ch.own(bands, y, c, own_sem, True).wait()
        for k in range(1, n):
            ch.copy(bands, y, c, k, send_sem, recv_sem, False, True).wait_recv()
            ch.copy(bands, y, c, k, send_sem, recv_sem, True, True).wait_send()
    keep.wait()
    give.wait()


def fourier_exchange(field, weight, forward, n, rows, log_start, rows_in, scale, collective_id):
    held, longitudes, half = field.shape
    orders, latitudes = log_start.shape
    degrees = weight.shape[0]
    ex = Exchange(n, held, True, False)
    chunks = held // CHUNK
    table = jax.ShapeDtypeStruct((orders, degrees * n, latitudes), jnp.bfloat16)
    return pl.pallas_call(
        functools.partial(fourier_kernel, ex, scale),
        out_shape=(
            jax.ShapeDtypeStruct((n * held, rows, half), field.dtype),
            table,
            table,
            jax.ShapeDtypeStruct((2, degrees, half, half), field.dtype),
        ),
        in_specs=[hbm_spec(), hbm_spec(), vmem_spec(), vmem_spec(), vmem_spec()],
        out_specs=(any_spec(), vmem_spec(), vmem_spec(), any_spec()),
        scratch_shapes=[
            pltpu.VMEM((orders, degrees * n, latitudes), jnp.float32),
            pltpu.VMEM((held, longitudes, half), field.dtype),
            pltpu.VMEM((held, n, rows, half), field.dtype),
            pltpu.SemaphoreType.DMA((chunks,)),
            pltpu.SemaphoreType.DMA((chunks, n)),
            pltpu.SemaphoreType.DMA((chunks, n)),
            pltpu.SemaphoreType.DMA((chunks,)),
            pltpu.SemaphoreType.DMA((3,)),
        ],
        compiler_params=params(collective_id),
        name="fourier_exchange",
    )(field, weight, forward, log_start, rows_in)


TILE = 128


def response_kernel(
    ex,
    grid,
    field,
    cotangent,
    inverse_t,
    inverse,
    output,
    y,
    held_field,
    held_cot,
    arrived,
    slopes,
    bands,
    load_sem,
    in_send,
    in_recv,
    in_own,
    out_send,
    out_recv,
    out_own,
    store_sem,
):
    n, ch = ex.n, Chunked(ex.n, ex.held)
    half = field.shape[2]
    tiles = field.shape[1] // TILE

    def part(ref, c):
        return ref.at[pl.ds(c * CHUNK, CHUNK)]

    def loads(c):
        return (
            pltpu.make_async_copy(part(field, c), part(held_field, c), load_sem.at[0, c]),
            pltpu.make_async_copy(part(cotangent, c), part(held_cot, c), load_sem.at[1, c]),
        )

    def store(c):
        return pltpu.make_async_copy(part(held_field, c), part(output, c), store_sem.at[c])

    for c in range(ch.chunks):
        for load in loads(c):
            load.start()
    ex.greet(False)
    for c in range(ch.chunks):
        for k in range(1, n):
            ch.copy(grid, arrived, c, k, in_send, in_recv, True, False).start()
        ch.own(grid, arrived, c, in_own, False).start()
    for c in range(ch.chunks):
        for load in loads(c):
            load.wait()
        ch.own(grid, arrived, c, in_own, False).wait()
        for k in range(1, n):
            ch.copy(grid, arrived, c, k, in_send, in_recv, False, False).wait_recv()

        def pair(i, carry, c=c):
            j = c * CHUNK + 2 * i
            wide = jnp.concatenate([flat(arrived[j]), flat(arrived[j + 1])], axis=1)

            def tile(t, inner):
                at = pl.ds(pl.multiple_of(t * TILE, TILE), TILE)
                response = mm(inverse_t[at, :], wide)
                cdf = 0.5 * (1.0 + lax.erf(response * (1.0 / math.sqrt(2.0))))
                density = jnp.exp(-0.5 * response * response) * (1.0 / math.sqrt(2.0 * math.pi))
                gain = response * cdf
                slope = cdf + response * density
                for side in range(2):
                    lanes = slice(side * half, (side + 1) * half)
                    base = held_field[j + side, at, :].astype(jnp.float32)
                    held_field[j + side, at, :] = (base + gain[:, lanes]).astype(jnp.bfloat16)
                    cot = held_cot[j + side, at, :].astype(jnp.float32)
                    slopes[at, lanes] = (cot * slope[:, lanes]).astype(jnp.bfloat16)
                return inner

            lax.fori_loop(0, tiles, tile, 0)
            out = mm(inverse[...], slopes[...])
            bands[j] = unflat(out[:, :half], n)
            bands[j + 1] = unflat(out[:, half:], n)
            return carry

        lax.fori_loop(0, CHUNK // 2, pair, 0)
        for k in range(1, n):
            ch.copy(bands, y, c, k, out_send, out_recv, True, True).start()
        ch.own(bands, y, c, out_own, True).start()
        store(c).start()
    for c in range(ch.chunks):
        ch.own(bands, y, c, out_own, True).wait()
        store(c).wait()
        for k in range(1, n):
            ch.copy(bands, y, c, k, out_send, out_recv, False, True).wait_recv()
            ch.copy(bands, y, c, k, out_send, out_recv, True, True).wait_send()
            ch.copy(grid, arrived, c, k, in_send, in_recv, True, False).wait_send()


def response_exchange(grid, field, cotangent, inverse_t, inverse, n, collective_id):
    held, longitudes, half = field.shape
    rows = grid.shape[1]
    chunks = held // CHUNK
    ex = Exchange(n, held, True, False)
    return pl.pallas_call(
        functools.partial(response_kernel, ex),
        out_shape=(
            jax.ShapeDtypeStruct(field.shape, field.dtype),
            jax.ShapeDtypeStruct((n * held, rows, half), field.dtype),
        ),
        in_specs=[any_spec(), hbm_spec(), hbm_spec()] + [vmem_spec()] * 2,
        out_specs=(any_spec(), any_spec()),
        scratch_shapes=[
            pltpu.VMEM((held, longitudes, half), field.dtype),
            pltpu.VMEM((held, longitudes, half), field.dtype),
            pltpu.VMEM((held, n, rows, half), field.dtype),
            pltpu.VMEM((longitudes, 2 * half), field.dtype),
            pltpu.VMEM((held, n, rows, half), field.dtype),
            pltpu.SemaphoreType.DMA((2, chunks)),
            pltpu.SemaphoreType.DMA((chunks, n)),
            pltpu.SemaphoreType.DMA((chunks, n)),
            pltpu.SemaphoreType.DMA((chunks,)),
            pltpu.SemaphoreType.DMA((chunks, n)),
            pltpu.SemaphoreType.DMA((chunks, n)),
            pltpu.SemaphoreType.DMA((chunks,)),
            pltpu.SemaphoreType.DMA((chunks,)),
        ],
        compiler_params=params(collective_id),
        name="response_exchange",
    )(grid, field, cotangent, inverse_t, inverse)


def field_grad_kernel(band, cotangent, forward_t, out):
    half = band.shape[-1]
    for i in range(0, band.shape[0], 2):
        wide = jnp.concatenate([flat(band[i]), flat(band[i + 1])], axis=1)
        total = mm(forward_t[...], wide)
        for side in range(2):
            part = total[:, side * half : (side + 1) * half]
            out[i + side] = (cotangent[i + side].astype(jnp.float32) + part).astype(out.dtype)


def final_field_grad(band, cotangent, forward_t):
    held, n, rows, half = band.shape
    longitudes = cotangent.shape[1]
    lat = pl.BlockSpec((2, longitudes, half), lambda i: (i, 0, 0))
    return pl.pallas_call(
        field_grad_kernel,
        grid=(held // 2,),
        out_shape=jax.ShapeDtypeStruct(cotangent.shape, cotangent.dtype),
        in_specs=[
            pl.BlockSpec((2, n, rows, half), lambda i: (i, 0, 0, 0)),
            lat,
            pl.BlockSpec(forward_t.shape, lambda i: (0, 0)),
        ],
        out_specs=lat,
        compiler_params=pltpu.CompilerParams(vmem_limit_bytes=24 * 2**20),
        name="field_grad",
    )(band, cotangent, forward_t)


def order_block(s):
    return s + ((s // 2) % 2) * (1 - 2 * (s % 2))


def holds(n, orders_at, degrees_at):
    return order_block(orders_at) + degrees_at >= n - 1


def degree_kernel(n, backward, scale, *refs):
    if backward:
        x, weights, coeffs, y, weight_grad, blocks = refs[:6]
    else:
        x, weights, y, blocks = refs[:4]
    mixed, zero, zero_sem, send1, recv1, own1, fsend, frecv, send2, recv2, own2 = refs[-11:]
    me = lax.axis_index("space")
    chan = lax.axis_index("chan")
    held, half = blocks.shape[1], blocks.shape[-1]
    mine = pl.ds(pl.multiple_of(chan * half, half), half)
    theirs = pl.ds(pl.multiple_of((1 - chan) * half, half), half)
    Exchange(n, held, False, True).greet(True)

    def ahead(k):
        return lax.rem(me + k, n)

    def behind(k):
        return lax.rem(me + n - k, n)

    def rows_of(ref, d):
        return ref.at[pl.ds(d * held, held)]

    def coming(k, sending):
        return pltpu.make_async_remote_copy(
            src_ref=rows_of(x, ahead(k)),
            dst_ref=blocks.at[0, :, me if sending else behind(k)],
            send_sem=send1.at[k],
            recv_sem=recv1.at[k],
            device_id={"space": ahead(k) if sending else behind(k)},
            device_id_type=MESH,
        )

    def across(k):
        return pltpu.make_async_remote_copy(
            src_ref=blocks.at[0, :, behind(k)],
            dst_ref=blocks.at[1, :, behind(k)],
            send_sem=fsend.at[k],
            recv_sem=frecv.at[k],
            device_id={"chan": 1 - chan},
            device_id_type=MESH,
        )

    def going(k, sending):
        return pltpu.make_async_remote_copy(
            src_ref=mixed.at[:, behind(k)],
            dst_ref=rows_of(y, me if sending else ahead(k)),
            send_sem=send2.at[k],
            recv_sem=recv2.at[k],
            device_id={"space": behind(k) if sending else ahead(k)},
            device_id_type=MESH,
        )

    def start_coming(k, carry):
        pl.when(holds(n, me, ahead(k)))(lambda: coming(k, True).start())
        return carry

    lax.fori_loop(1, n, start_coming, 0)
    own_in = pltpu.make_async_copy(rows_of(x, me), blocks.at[0, :, me], own1)
    own_out = pltpu.make_async_copy(mixed.at[:, me], rows_of(y, me), own2)
    zero[...] = jnp.zeros_like(zero)

    def zeros_of(k):
        return pltpu.make_async_copy(zero, rows_of(y, ahead(k)), zero_sem.at[k])

    def fill(k, carry):
        other = behind(k)

        @pl.when(jnp.logical_not(holds(n, other, me)))
        def _():
            for side in range(2):
                for at in range(held):
                    blocks[side, at, other] = jnp.zeros(blocks.shape[3:], blocks.dtype)

        pl.when(jnp.logical_not(holds(n, me, ahead(k))))(lambda: zeros_of(k).start())
        return carry

    def mix(other):
        for at in range(held):
            wide = jnp.concatenate([blocks[0, at, other], blocks[1, at, other]], axis=1)
            if backward:
                weight = jnp.concatenate([weights[0, at], weights[1, at]], axis=1)
                total = lax.dot_general(
                    wide, weight, (((1,), (1,)), ((), ())), preferred_element_type=jnp.float32
                )
            else:
                weight = jnp.concatenate([weights[at, mine, :], weights[at, theirs, :]], axis=0)
                total = mm(wide, weight)
            mixed[at, other] = (total * scale).astype(mixed.dtype)

    has_own = holds(n, me, me)

    @pl.when(has_own)
    def _():
        own_in.start()
        own_in.wait()
        across(0).start()

    lax.fori_loop(0, n, fill, 0)

    def settle(k):
        across(k).wait_recv()
        mix(behind(k))
        going(k, True).start()

    def turn(k, carry):
        @pl.when(holds(n, behind(k), me))
        def _():
            coming(k, False).wait_recv()
            across(k).start()

        @pl.when(jnp.logical_and(k > 1, holds(n, behind(k - 1), me)))
        def _():
            settle(k - 1)

        return carry

    lax.fori_loop(1, n, turn, 0)
    pl.when(holds(n, behind(n - 1), me))(lambda: settle(n - 1))

    @pl.when(has_own)
    def _():
        across(0).wait_recv()
        mix(me)
        own_out.start()

    if backward:

        def products(at, carry):
            grad = flat(blocks[0, at])
            for side, lines in ((0, mine), (1, theirs)):
                part = lax.dot_general(
                    flat(coeffs[side, at]),
                    grad,
                    (((0,), (0,)), ((), ())),
                    preferred_element_type=jnp.float32,
                )
                weight_grad[at, lines, :] = (part * scale).astype(weight_grad.dtype)
            return carry

        lax.fori_loop(0, held, products, 0)

    @pl.when(has_own)
    def _():
        own_out.wait()
        across(0).wait_send()

    def finish(k, carry):
        @pl.when(holds(n, behind(k), me))
        def _():
            across(k).wait_send()
            going(k, True).wait_send()

        @pl.when(holds(n, me, ahead(k)))
        def _():
            coming(k, True).wait_send()
            going(k, False).wait_recv()

        return carry

    lax.fori_loop(1, n, finish, 0)

    def filled(k, carry):
        pl.when(jnp.logical_not(holds(n, me, ahead(k))))(lambda: zeros_of(k).wait())
        return carry

    lax.fori_loop(0, n, filled, 0)


def degree_exchange(x, weights, n, scale, collective_id, coeffs=None):
    total, rows, half = x.shape
    held = total // n
    backward = coeffs is not None
    block = jax.ShapeDtypeStruct((2, held, n, rows, half), x.dtype)
    shapes = [jax.ShapeDtypeStruct(x.shape, x.dtype)]
    specs = [any_spec(), vmem_spec()]
    scratch = []
    if backward:
        shapes.append(jax.ShapeDtypeStruct((held, 2 * half, half), x.dtype))
        scratch.append(pltpu.VMEM(block.shape, x.dtype))
    else:
        shapes.append(block)
    dma = pltpu.SemaphoreType.DMA
    return pl.pallas_call(
        functools.partial(degree_kernel, n, backward, scale),
        out_shape=tuple(shapes),
        in_specs=[any_spec()] + [vmem_spec()] * (2 if backward else 1),
        out_specs=tuple(specs),
        scratch_shapes=scratch
        + [
            pltpu.VMEM((held, n, rows, half), x.dtype),
            pltpu.VMEM((held, rows, half), x.dtype),
            dma((n,)),
            dma((n,)),
            dma((n,)),
            dma,
            dma((n,)),
            dma((n,)),
            dma((n,)),
            dma((n,)),
            dma,
        ],
        compiler_params=params(collective_id),
        name="degree_exchange",
    )(*([x, weights] + ([coeffs] if backward else [])))


def dot32(formula, left, right):
    return jnp.einsum(formula, left, right, preferred_element_type=jnp.float32)


def local(field, spectral_weight, cotangent):
    n = lax.axis_size("space")
    held, longitudes, half = field.shape
    degrees_held, channels, _ = spectral_weight.shape
    latitudes = held * n
    degrees = degrees_held * n
    orders_held = degrees_held
    rows = 2 * orders_held
    mix_scale = 1.0 / math.sqrt(channels)
    chan = lax.axis_index("chan")
    block = n - 1 - order_block(lax.axis_index("space"))
    held_blocks = [n - 1 - order_block(s) for s in range(n)]
    order_list = np.arange(degrees).reshape(n, orders_held)[held_blocks].reshape(-1)
    forward_np, inverse_np = fourier_tables(longitudes, order_list)
    forward, inverse = jnp.asarray(forward_np), jnp.asarray(inverse_np)
    log_np, rows_np, scale = latitude_rows(latitudes, longitudes, degrees)
    log_start = lax.dynamic_slice_in_dim(jnp.asarray(log_np), block * orders_held, orders_held, 0)

    by_order, analysis, synthesis, weights = fourier_exchange(
        field, spectral_weight, forward, n, rows, log_start, jnp.asarray(rows_np), scale, 0
    )

    def to_degrees(table, values):
        values = values.reshape(latitudes, orders_held, 2, half)
        out = dot32("mlj,jmrc->lmrc", table, values).astype(jnp.bfloat16)
        return out.reshape(degrees, rows, half)

    def to_latitudes(table, values):
        values = values.reshape(degrees, orders_held, 2, half)
        out = dot32("mlj,lmrc->jmrc", table, values).astype(jnp.bfloat16)
        return out.reshape(latitudes, rows, half)

    mixed_orders, coeffs = degree_exchange(
        to_degrees(analysis, by_order), spectral_weight, n, mix_scale, 1
    )
    output, grad_by_order = response_exchange(
        to_latitudes(synthesis, mixed_orders),
        field,
        cotangent,
        jnp.asarray(np.ascontiguousarray(inverse_np.T)),
        inverse,
        n,
        3,
    )
    coeff_orders, weight_grad = degree_exchange(
        to_degrees(synthesis, grad_by_order), weights, n, mix_scale, 5, coeffs
    )
    fourier_band = swap(to_latitudes(analysis, coeff_orders), n, False, False, 7)
    field_grad = final_field_grad(
        fourier_band, cotangent, jnp.asarray(np.ascontiguousarray(forward_np.T))
    )
    return (output, field_grad, weight_grad)


def solution(mesh):
    in_specs = (
        P(("parts", "space"), None, "chan"),
        P("space", None, "chan"),
        P(("parts", "space"), None, "chan"),
    )
    out_specs = (
        P(("parts", "space"), None, "chan"),
        P(("parts", "space"), None, "chan"),
        P(("parts", "space"), None, "chan"),
    )
    return jax.shard_map(local, mesh=mesh, in_specs=in_specs, out_specs=out_specs, check_vma=False)
```

```python
import functools
import math

import jax
import jax.numpy as jnp
import ml_dtypes
import numpy as np
from jax import lax
from jax.experimental import pallas as pl
from jax.experimental.pallas import tpu as pltpu
from jax.sharding import PartitionSpec as P

LIMIT = 2.0**40
SHRINK = 2.0 ** (-40)
LOGSTEP = 40.0 * math.log(2.0)
MESH = pl.DeviceIdType.MESH


def fourier_tables(longitudes, order_list):
    products = (np.asarray(order_list)[:, None] * np.arange(longitudes)[None, :]) % longitudes
    angle = 2.0 * math.pi / longitudes * products
    table = np.stack([np.cos(angle), -np.sin(angle)], axis=1)
    weights = np.where(np.asarray(order_list) == 0, 1.0, 2.0)[:, None, None]
    forward = table.reshape(-1, longitudes).astype(np.float32)
    inverse = (table * weights).reshape(-1, longitudes).astype(np.float32)
    return forward.astype(ml_dtypes.bfloat16), inverse.astype(ml_dtypes.bfloat16)


def latitude_rows(latitudes, longitudes, orders):
    half = latitudes // 2
    north = (np.arange(half) + 0.5) * (math.pi / latitudes)
    cosines = np.concatenate([np.cos(north), -np.cos(north)[::-1]])
    sines = np.concatenate([np.sin(north), np.sin(north)[::-1]])
    order = np.arange(orders)
    gammas = np.array([math.lgamma(m + 0.5) - math.lgamma(m + 1.0) for m in order])
    start = 0.5 * (np.log((2.0 * order + 1.0) / (4.0 * math.pi)) + gammas - 0.5 * math.log(math.pi))
    log_start = start[:, None] + order[:, None] * np.log(sines)[None, :]
    area = latitudes * longitudes
    rows = np.stack([cosines, math.pi**1.5 / math.sqrt(area) * sines])
    return (
        log_start.astype(np.float32),
        rows.astype(np.float32),
        math.sqrt(4.0 * math.pi / area),
    )


def legendre_into(log_start, rows, synthesis_scale, first_order, values, analysis, synthesis):
    held, degrees, latitudes = values.shape
    shape = (held, latitudes)
    order = (lax.broadcasted_iota(jnp.int32, shape, 0) + first_order).astype(jnp.float32)
    cosines = jnp.broadcast_to(rows[0:1, :], shape)
    start = log_start[...]

    def step(at, state):
        previous, before, rescales = state
        degree = at.astype(jnp.float32)
        lower_deg = degree - 1.0
        square = order * order
        upper = jnp.sqrt((4.0 * degree * degree - 1.0) / jnp.maximum(degree * degree - square, 1.0))
        lower = jnp.sqrt(
            jnp.maximum(lower_deg * lower_deg - square, 0.0)
            / jnp.maximum(4.0 * lower_deg * lower_deg - 1.0, 1.0)
        )
        newest = jnp.where(
            degree == order,
            1.0,
            jnp.where(degree > order, upper * (cosines * previous - lower * before), 0.0),
        )
        too_large = jnp.abs(newest) > LIMIT
        newest = jnp.where(too_large, newest * SHRINK, newest)
        previous = jnp.where(too_large, previous * SHRINK, previous)
        rescales = rescales + jnp.where(too_large, 1.0, 0.0)
        values[:, pl.ds(at, 1), :] = (newest * jnp.exp(start + rescales * LOGSTEP))[:, None, :]
        return newest, previous, rescales

    zero = jnp.zeros(shape, jnp.float32)
    lax.fori_loop(0, degrees, step, (zero, zero, zero))
    quadrature = rows[1:2, :]

    def finish(m, carry):
        analysis[m] = (values[m] * quadrature).astype(jnp.bfloat16)
        synthesis[m] = (values[m] * synthesis_scale).astype(jnp.bfloat16)
        return carry

    lax.fori_loop(0, held, finish, 0)


class Exchange:
    def __init__(self, n, held, spread, sparse):
        self.n, self.held, self.spread, self.sparse = n, held, spread, sparse

    def greet(self, chan):
        self.signal(chan)
        self.hear(chan)

    def hear(self, chan):
        pl.semaphore_wait(pltpu.get_barrier_semaphore(), self.n - 1 + (1 if chan else 0))

    def signal(self, chan):
        me = lax.axis_index("space")
        barrier = pltpu.get_barrier_semaphore()
        for k in range(1, self.n):
            pl.semaphore_signal(
                barrier, inc=1, device_id={"space": lax.rem(me + k, self.n)}, device_id_type=MESH
            )
        if chan:
            pl.semaphore_signal(
                barrier, inc=1, device_id={"chan": 1 - lax.axis_index("chan")}, device_id_type=MESH
            )

    def source(self, x, d):
        return x.at[:, d] if self.spread else x.at[pl.ds(d * self.held, self.held)]

    def slot(self, y, s):
        return y.at[pl.ds(s * self.held, self.held)] if self.spread else y.at[:, s]

    def when(self, other, run):
        if self.sparse:
            pl.when(lax.axis_index("space") + other >= self.n - 1)(run)
        else:
            run()

    def copy(self, x, y, k, send_sem, recv_sem, sending):
        me = lax.axis_index("space")
        other = lax.rem(me + k, self.n) if sending else lax.rem(me + self.n - k, self.n)
        return other, pltpu.make_async_remote_copy(
            src_ref=self.source(x, other),
            dst_ref=self.slot(y, me if sending else other),
            send_sem=send_sem.at[k],
            recv_sem=recv_sem.at[k],
            device_id={"space": other},
            device_id_type=MESH,
        )


def send_all(ex, x, y, send_sem, recv_sem):
    for k in range(1, ex.n):
        other, copy = ex.copy(x, y, k, send_sem, recv_sem, True)
        ex.when(other, copy.start)


def wait_sends(ex, x, y, send_sem, recv_sem):
    for k in range(1, ex.n):
        other, copy = ex.copy(x, y, k, send_sem, recv_sem, True)
        ex.when(other, copy.wait_send)


def zero_fill(ex, targets, zero, zero_sem, start):
    me = lax.axis_index("space")
    for k in range(ex.n):
        other = lax.rem(me + ex.n - k, ex.n)

        @pl.when(me + other < ex.n - 1)
        def _():
            for i, y in enumerate(targets):
                copy = pltpu.make_async_copy(zero, ex.slot(y, other), zero_sem.at[i, k])
                copy.start() if start else copy.wait()


def plain_kernel(ex, *refs):
    if ex.sparse:
        x, y, zero, zero_sem, send_sem, recv_sem, own_sem = refs
    else:
        x, y, send_sem, recv_sem, own_sem = refs
    me = lax.axis_index("space")
    ex.greet(False)
    send_all(ex, x, y, send_sem, recv_sem)
    own = pltpu.make_async_copy(ex.source(x, me), ex.slot(y, me), own_sem)
    ex.when(me, own.start)
    if ex.sparse:
        zero[...] = jnp.zeros_like(zero)
        zero_fill(ex, [y], zero, zero_sem, True)
    ex.when(me, own.wait)
    for k in range(1, ex.n):
        other, copy = ex.copy(x, y, k, send_sem, recv_sem, False)
        ex.when(other, copy.wait_recv)
    wait_sends(ex, x, y, send_sem, recv_sem)
    if ex.sparse:
        zero_fill(ex, [y], zero, zero_sem, False)


def any_spec():
    return pl.BlockSpec(memory_space=pl.ANY)


def hbm_spec():
    return pl.BlockSpec(memory_space=pltpu.HBM)


def vmem_spec():
    return pl.BlockSpec(memory_space=pltpu.VMEM)


def params(collective_id, mebibytes=24):
    return pltpu.CompilerParams(
        collective_id=collective_id, has_side_effects=True, vmem_limit_bytes=mebibytes * 2**20
    )


def swap(x, n, spread, sparse, collective_id):
    if spread:
        held, _, rows, width = x.shape
        shape = (n * held, rows, width)
    else:
        total, rows, width = x.shape
        held = total // n
        shape = (held, n, rows, width)
    ex = Exchange(n, held, spread, sparse)
    sems = [
        pltpu.SemaphoreType.DMA((n,)),
        pltpu.SemaphoreType.DMA((n,)),
        pltpu.SemaphoreType.DMA,
    ]
    out = jax.ShapeDtypeStruct(shape, x.dtype)
    scratch = list(sems)
    if sparse:
        zeros = [pltpu.VMEM((held, rows, width), x.dtype), pltpu.SemaphoreType.DMA((1, n))]
        scratch = zeros + scratch
    return pl.pallas_call(
        functools.partial(plain_kernel, ex),
        out_shape=out,
        in_specs=[any_spec()],
        out_specs=any_spec(),
        scratch_shapes=scratch,
        compiler_params=params(collective_id),
        name="exchange",
    )(x)


def flat(block):
    rows = block.shape[0] * block.shape[1]
    return block.astype(jnp.float32).reshape(rows, block.shape[2]).astype(block.dtype)


def unflat(values, n):
    return values.reshape(n, values.shape[0] // n, values.shape[1]).astype(jnp.bfloat16)


def mm(left, right):
    return jnp.dot(left, right, preferred_element_type=jnp.float32)


CHUNK = 4


class Chunked:
    def __init__(self, n, held):
        self.n, self.held = n, held
        self.chunks = held // CHUNK

    def band(self, f, c, d):
        return f.at[pl.ds(c * CHUNK, CHUNK), d]

    def lats(self, y, c, s):
        return y.at[pl.ds(s * self.held + c * CHUNK, CHUNK)]

    def copy(self, x, y, c, k, send_sem, recv_sem, sending, outward):
        me = lax.axis_index("space")
        other = lax.rem(me + k, self.n) if sending else lax.rem(me + self.n - k, self.n)
        here = me if sending else other
        if outward:
            src, dst = self.band(x, c, other), self.lats(y, c, here)
        else:
            src, dst = self.lats(x, c, other), self.band(y, c, here)
        return pltpu.make_async_remote_copy(
            src_ref=src,
            dst_ref=dst,
            send_sem=send_sem.at[c, k],
            recv_sem=recv_sem.at[c, k],
            device_id={"space": other},
            device_id_type=MESH,
        )

    def own(self, x, y, c, sem, outward):
        me = lax.axis_index("space")
        if outward:
            return pltpu.make_async_copy(self.band(x, c, me), self.lats(y, c, me), sem.at[c])
        return pltpu.make_async_copy(self.lats(x, c, me), self.band(y, c, me), sem.at[c])


def fourier_kernel(
    ex,
    synthesis_scale,
    field,
    weight,
    forward_in,
    starts_in,
    y,
    analysis,
    synthesis,
    weights,
    values,
    forward,
    starts,
    held_field,
    bands,
    table_sem,
    load_sem,
    send_sem,
    recv_sem,
    own_sem,
    weight_sem,
):
    n, ch = ex.n, Chunked(ex.n, ex.held)
    me = lax.axis_index("space")
    chan = lax.axis_index("chan")
    half = weight.shape[2]
    loads = [
        pltpu.make_async_copy(
            field.at[pl.ds(c * CHUNK, CHUNK)], held_field.at[pl.ds(c * CHUNK, CHUNK)], load_sem.at[c]
        )
        for c in range(ch.chunks)
    ]
    load_forward = pltpu.make_async_copy(forward_in, forward, table_sem.at[0])
    load_starts = pltpu.make_async_copy(starts_in, starts, table_sem.at[1])
    load_forward.start()
    for load in loads:
        load.start()
    load_starts.start()
    ex.signal(True)
    load_forward.wait()
    keep = pltpu.make_async_copy(
        weight.at[:, pl.ds(pl.multiple_of(chan * half, half), half)], weights.at[0], weight_sem.at[0]
    )
    give = pltpu.make_async_remote_copy(
        src_ref=weight.at[:, pl.ds(pl.multiple_of((1 - chan) * half, half), half)],
        dst_ref=weights.at[1],
        send_sem=weight_sem.at[1],
        recv_sem=weight_sem.at[2],
        device_id={"chan": 1 - chan},
        device_id_type=MESH,
    )
    for c in range(ch.chunks):
        loads[c].wait()

        def pair(i, carry, c=c):
            j = c * CHUNK + 2 * i
            wide = jnp.concatenate([held_field[j], held_field[j + 1]], axis=1)
            out = mm(forward[...], wide)
            bands[j] = unflat(out[:, :half], n)
            bands[j + 1] = unflat(out[:, half:], n)
            return carry

        lax.fori_loop(0, CHUNK // 2, pair, 0)
        if c == 0:
            ex.hear(True)
        for k in range(1, n):
            ch.copy(bands, y, c, k, send_sem, recv_sem, True, True).start()
        ch.own(bands, y, c, own_sem, True).start()
    keep.start()
    give.start()
    load_starts.wait()
    block = n - 1 - order_block(me)
    legendre_into(
        starts.at[block],
        starts.at[n],
        synthesis_scale,
        block * analysis.shape[0],
        values,
        analysis,
        synthesis,
    )
    for c in range(ch.chunks):
        ch.own(bands, y, c, own_sem, True).wait()
        for k in range(1, n):
            ch.copy(bands, y, c, k, send_sem, recv_sem, False, True).wait_recv()
            ch.copy(bands, y, c, k, send_sem, recv_sem, True, True).wait_send()
    keep.wait()
    give.wait()


def fourier_exchange(field, weight, forward, n, rows, starts, scale, collective_id):
    held, longitudes, half = field.shape
    _, orders, latitudes = starts.shape
    degrees = weight.shape[0]
    ex = Exchange(n, held, True, False)
    chunks = held // CHUNK
    table = jax.ShapeDtypeStruct((orders, degrees * n, latitudes), jnp.bfloat16)
    return pl.pallas_call(
        functools.partial(fourier_kernel, ex, scale),
        out_shape=(
            jax.ShapeDtypeStruct((n * held, rows, half), field.dtype),
            table,
            table,
            jax.ShapeDtypeStruct((2, degrees, half, half), field.dtype),
        ),
        in_specs=[hbm_spec()] * 4,
        out_specs=(any_spec(), vmem_spec(), vmem_spec(), any_spec()),
        scratch_shapes=[
            pltpu.VMEM((orders, degrees * n, latitudes), jnp.float32),
            pltpu.VMEM(forward.shape, forward.dtype),
            pltpu.VMEM(starts.shape, starts.dtype),
            pltpu.VMEM((held, longitudes, half), field.dtype),
            pltpu.VMEM((held, n, rows, half), field.dtype),
            pltpu.SemaphoreType.DMA((2,)),
            pltpu.SemaphoreType.DMA((chunks,)),
            pltpu.SemaphoreType.DMA((chunks, n)),
            pltpu.SemaphoreType.DMA((chunks, n)),
            pltpu.SemaphoreType.DMA((chunks,)),
            pltpu.SemaphoreType.DMA((3,)),
        ],
        compiler_params=params(collective_id, 60),
        name="fourier_exchange",
    )(field, weight, forward, starts)


TILE = 128


def response_kernel(
    ex,
    grid,
    field,
    cotangent,
    inverse_t,
    inverse,
    output,
    y,
    held_field,
    held_cot,
    arrived,
    slopes,
    bands,
    load_sem,
    in_send,
    in_recv,
    in_own,
    out_send,
    out_recv,
    out_own,
    store_sem,
):
    n, ch = ex.n, Chunked(ex.n, ex.held)
    half = field.shape[2]
    tiles = field.shape[1] // TILE

    def part(ref, c):
        return ref.at[pl.ds(c * CHUNK, CHUNK)]

    def loads(c):
        return (
            pltpu.make_async_copy(part(field, c), part(held_field, c), load_sem.at[0, c]),
            pltpu.make_async_copy(part(cotangent, c), part(held_cot, c), load_sem.at[1, c]),
        )

    def store(c):
        return pltpu.make_async_copy(part(held_field, c), part(output, c), store_sem.at[c])

    for c in range(ch.chunks):
        for load in loads(c):
            load.start()
    ex.greet(False)
    for c in range(ch.chunks):
        for k in range(1, n):
            ch.copy(grid, arrived, c, k, in_send, in_recv, True, False).start()
        ch.own(grid, arrived, c, in_own, False).start()
    for c in range(ch.chunks):
        for load in loads(c):
            load.wait()
        ch.own(grid, arrived, c, in_own, False).wait()
        for k in range(1, n):
            ch.copy(grid, arrived, c, k, in_send, in_recv, False, False).wait_recv()

        def pair(i, carry, c=c):
            j = c * CHUNK + 2 * i
            wide = jnp.concatenate([flat(arrived[j]), flat(arrived[j + 1])], axis=1)

            def tile(t, inner):
                at = pl.ds(pl.multiple_of(t * TILE, TILE), TILE)
                response = mm(inverse_t[at, :], wide)
                cdf = 0.5 * (1.0 + lax.erf(response * (1.0 / math.sqrt(2.0))))
                density = jnp.exp(-0.5 * response * response) * (1.0 / math.sqrt(2.0 * math.pi))
                gain = response * cdf
                slope = cdf + response * density
                for side in range(2):
                    lanes = slice(side * half, (side + 1) * half)
                    base = held_field[j + side, at, :].astype(jnp.float32)
                    held_field[j + side, at, :] = (base + gain[:, lanes]).astype(jnp.bfloat16)
                    cot = held_cot[j + side, at, :].astype(jnp.float32)
                    slopes[at, lanes] = (cot * slope[:, lanes]).astype(jnp.bfloat16)
                return inner

            lax.fori_loop(0, tiles, tile, 0)
            out = mm(inverse[...], slopes[...])
            bands[j] = unflat(out[:, :half], n)
            bands[j + 1] = unflat(out[:, half:], n)
            return carry

        lax.fori_loop(0, CHUNK // 2, pair, 0)
        for k in range(1, n):
            ch.copy(bands, y, c, k, out_send, out_recv, True, True).start()
        ch.own(bands, y, c, out_own, True).start()
        store(c).start()
    for c in range(ch.chunks):
        ch.own(bands, y, c, out_own, True).wait()
        store(c).wait()
        for k in range(1, n):
            ch.copy(bands, y, c, k, out_send, out_recv, False, True).wait_recv()
            ch.copy(bands, y, c, k, out_send, out_recv, True, True).wait_send()
            ch.copy(grid, arrived, c, k, in_send, in_recv, True, False).wait_send()


def response_exchange(grid, field, cotangent, inverse_t, inverse, n, collective_id):
    held, longitudes, half = field.shape
    rows = grid.shape[1]
    chunks = held // CHUNK
    ex = Exchange(n, held, True, False)
    return pl.pallas_call(
        functools.partial(response_kernel, ex),
        out_shape=(
            jax.ShapeDtypeStruct(field.shape, field.dtype),
            jax.ShapeDtypeStruct((n * held, rows, half), field.dtype),
        ),
        in_specs=[any_spec(), hbm_spec(), hbm_spec()] + [vmem_spec()] * 2,
        out_specs=(any_spec(), any_spec()),
        scratch_shapes=[
            pltpu.VMEM((held, longitudes, half), field.dtype),
            pltpu.VMEM((held, longitudes, half), field.dtype),
            pltpu.VMEM((held, n, rows, half), field.dtype),
            pltpu.VMEM((longitudes, 2 * half), field.dtype),
            pltpu.VMEM((held, n, rows, half), field.dtype),
            pltpu.SemaphoreType.DMA((2, chunks)),
            pltpu.SemaphoreType.DMA((chunks, n)),
            pltpu.SemaphoreType.DMA((chunks, n)),
            pltpu.SemaphoreType.DMA((chunks,)),
            pltpu.SemaphoreType.DMA((chunks, n)),
            pltpu.SemaphoreType.DMA((chunks, n)),
            pltpu.SemaphoreType.DMA((chunks,)),
            pltpu.SemaphoreType.DMA((chunks,)),
        ],
        compiler_params=params(collective_id),
        name="response_exchange",
    )(grid, field, cotangent, inverse_t, inverse)


def field_grad_kernel(
    band, cotangent, forward_t, output, weight_grad, out, output_out, weight_out, sem
):
    half = band.shape[-1]
    passing = [
        pltpu.make_async_copy(output, output_out, sem.at[0]),
        pltpu.make_async_copy(weight_grad, weight_out, sem.at[1]),
    ]

    @pl.when(pl.program_id(0) == 0)
    def _():
        for copy in passing:
            copy.start()

    for i in range(0, band.shape[0], 2):
        wide = jnp.concatenate([flat(band[i]), flat(band[i + 1])], axis=1)
        total = mm(forward_t[...], wide)
        for side in range(2):
            part = total[:, side * half : (side + 1) * half]
            out[i + side] = (cotangent[i + side].astype(jnp.float32) + part).astype(out.dtype)

    @pl.when(pl.program_id(0) == pl.num_programs(0) - 1)
    def _():
        for copy in passing:
            copy.wait()


def final_field_grad(band, cotangent, forward_t, output, weight_grad):
    held, n, rows, half = band.shape
    longitudes = cotangent.shape[1]
    lat = pl.BlockSpec((2, longitudes, half), lambda i: (i, 0, 0))
    return pl.pallas_call(
        field_grad_kernel,
        grid=(held // 2,),
        out_shape=tuple(
            jax.ShapeDtypeStruct(like.shape, like.dtype) for like in (cotangent, output, weight_grad)
        ),
        in_specs=[
            pl.BlockSpec((2, n, rows, half), lambda i: (i, 0, 0, 0)),
            lat,
            pl.BlockSpec(forward_t.shape, lambda i: (0, 0)),
            any_spec(),
            any_spec(),
        ],
        out_specs=(lat, any_spec(), any_spec()),
        scratch_shapes=[pltpu.SemaphoreType.DMA((2,))],
        compiler_params=pltpu.CompilerParams(vmem_limit_bytes=24 * 2**20),
        name="field_grad",
    )(band, cotangent, forward_t, output, weight_grad)


def order_block(s):
    return s + ((s // 2) % 2) * (1 - 2 * (s % 2))


def holds(n, orders_at, degrees_at):
    return order_block(orders_at) + degrees_at >= n - 1


def degree_kernel(n, backward, scale, *refs):
    if backward:
        x, weights, coeffs, y, weight_grad, blocks = refs[:6]
    else:
        x, weights, y, blocks = refs[:4]
    mixed, zero, zero_sem, send1, recv1, own1, fsend, frecv, send2, recv2, own2 = refs[-11:]
    me = lax.axis_index("space")
    chan = lax.axis_index("chan")
    held, half = blocks.shape[1], blocks.shape[-1]
    mine = pl.ds(pl.multiple_of(chan * half, half), half)
    theirs = pl.ds(pl.multiple_of((1 - chan) * half, half), half)
    Exchange(n, held, False, True).greet(True)

    def ahead(k):
        return lax.rem(me + k, n)

    def behind(k):
        return lax.rem(me + n - k, n)

    def rows_of(ref, d):
        return ref.at[pl.ds(d * held, held)]

    def coming(k, sending):
        return pltpu.make_async_remote_copy(
            src_ref=rows_of(x, ahead(k)),
            dst_ref=blocks.at[0, :, me if sending else behind(k)],
            send_sem=send1.at[k],
            recv_sem=recv1.at[k],
            device_id={"space": ahead(k) if sending else behind(k)},
            device_id_type=MESH,
        )

    def across(k):
        return pltpu.make_async_remote_copy(
            src_ref=blocks.at[0, :, behind(k)],
            dst_ref=blocks.at[1, :, behind(k)],
            send_sem=fsend.at[k],
            recv_sem=frecv.at[k],
            device_id={"chan": 1 - chan},
            device_id_type=MESH,
        )

    def going(k, sending):
        return pltpu.make_async_remote_copy(
            src_ref=mixed.at[:, behind(k)],
            dst_ref=rows_of(y, me if sending else ahead(k)),
            send_sem=send2.at[k],
            recv_sem=recv2.at[k],
            device_id={"space": behind(k) if sending else ahead(k)},
            device_id_type=MESH,
        )

    def start_coming(k, carry):
        pl.when(holds(n, me, ahead(k)))(lambda: coming(k, True).start())
        return carry

    lax.fori_loop(1, n, start_coming, 0)
    own_in = pltpu.make_async_copy(rows_of(x, me), blocks.at[0, :, me], own1)
    own_out = pltpu.make_async_copy(mixed.at[:, me], rows_of(y, me), own2)
    zero[...] = jnp.zeros_like(zero)

    def zeros_of(k):
        return pltpu.make_async_copy(zero, rows_of(y, ahead(k)), zero_sem.at[k])

    def fill(k, carry):
        other = behind(k)

        @pl.when(jnp.logical_not(holds(n, other, me)))
        def _():
            for side in range(2):
                for at in range(held):
                    blocks[side, at, other] = jnp.zeros(blocks.shape[3:], blocks.dtype)

        pl.when(jnp.logical_not(holds(n, me, ahead(k))))(lambda: zeros_of(k).start())
        return carry

    def mix(other):
        for at in range(held):
            wide = jnp.concatenate([blocks[0, at, other], blocks[1, at, other]], axis=1)
            if backward:
                weight = jnp.concatenate([weights[0, at], weights[1, at]], axis=1)
                total = lax.dot_general(
                    wide, weight, (((1,), (1,)), ((), ())), preferred_element_type=jnp.float32
                )
            else:
                weight = jnp.concatenate([weights[at, mine, :], weights[at, theirs, :]], axis=0)
                total = mm(wide, weight)
            mixed[at, other] = (total * scale).astype(mixed.dtype)

    has_own = holds(n, me, me)

    @pl.when(has_own)
    def _():
        own_in.start()
        own_in.wait()
        across(0).start()

    lax.fori_loop(0, n, fill, 0)

    def settle(k):
        across(k).wait_recv()
        mix(behind(k))
        going(k, True).start()

    def turn(k, carry):
        @pl.when(holds(n, behind(k), me))
        def _():
            coming(k, False).wait_recv()
            across(k).start()

        @pl.when(jnp.logical_and(k > 1, holds(n, behind(k - 1), me)))
        def _():
            settle(k - 1)

        return carry

    lax.fori_loop(1, n, turn, 0)
    pl.when(holds(n, behind(n - 1), me))(lambda: settle(n - 1))

    @pl.when(has_own)
    def _():
        across(0).wait_recv()
        mix(me)
        own_out.start()

    if backward:

        def products(at, carry):
            grad = flat(blocks[0, at])
            for side, lines in ((0, mine), (1, theirs)):
                part = lax.dot_general(
                    flat(coeffs[side, at]),
                    grad,
                    (((0,), (0,)), ((), ())),
                    preferred_element_type=jnp.float32,
                )
                weight_grad[at, lines, :] = (part * scale).astype(weight_grad.dtype)
            return carry

        lax.fori_loop(0, held, products, 0)

    @pl.when(has_own)
    def _():
        own_out.wait()
        across(0).wait_send()

    def finish(k, carry):
        @pl.when(holds(n, behind(k), me))
        def _():
            across(k).wait_send()
            going(k, True).wait_send()

        @pl.when(holds(n, me, ahead(k)))
        def _():
            coming(k, True).wait_send()
            going(k, False).wait_recv()

        return carry

    lax.fori_loop(1, n, finish, 0)

    def filled(k, carry):
        pl.when(jnp.logical_not(holds(n, me, ahead(k))))(lambda: zeros_of(k).wait())
        return carry

    lax.fori_loop(0, n, filled, 0)


def degree_exchange(x, weights, n, scale, collective_id, coeffs=None):
    total, rows, half = x.shape
    held = total // n
    backward = coeffs is not None
    block = jax.ShapeDtypeStruct((2, held, n, rows, half), x.dtype)
    shapes = [jax.ShapeDtypeStruct(x.shape, x.dtype)]
    specs = [any_spec(), vmem_spec()]
    scratch = []
    if backward:
        shapes.append(jax.ShapeDtypeStruct((held, 2 * half, half), x.dtype))
        scratch.append(pltpu.VMEM(block.shape, x.dtype))
    else:
        shapes.append(block)
    dma = pltpu.SemaphoreType.DMA
    return pl.pallas_call(
        functools.partial(degree_kernel, n, backward, scale),
        out_shape=tuple(shapes),
        in_specs=[any_spec()] + [vmem_spec()] * (2 if backward else 1),
        out_specs=tuple(specs),
        scratch_shapes=scratch
        + [
            pltpu.VMEM((held, n, rows, half), x.dtype),
            pltpu.VMEM((held, rows, half), x.dtype),
            dma((n,)),
            dma((n,)),
            dma((n,)),
            dma,
            dma((n,)),
            dma((n,)),
            dma((n,)),
            dma((n,)),
            dma,
        ],
        compiler_params=params(collective_id),
        name="degree_exchange",
    )(*([x, weights] + ([coeffs] if backward else [])))


def dot32(formula, left, right):
    return jnp.einsum(formula, left, right, preferred_element_type=jnp.float32)


def local(field, spectral_weight, cotangent):
    n = lax.axis_size("space")
    held, longitudes, half = field.shape
    degrees_held, channels, _ = spectral_weight.shape
    latitudes = held * n
    degrees = degrees_held * n
    orders_held = degrees_held
    rows = 2 * orders_held
    mix_scale = 1.0 / math.sqrt(channels)
    chan = lax.axis_index("chan")
    held_blocks = [n - 1 - order_block(s) for s in range(n)]
    order_list = np.arange(degrees).reshape(n, orders_held)[held_blocks].reshape(-1)
    forward_np, inverse_np = fourier_tables(longitudes, order_list)
    forward, inverse = jnp.asarray(forward_np), jnp.asarray(inverse_np)
    log_np, rows_np, scale = latitude_rows(latitudes, longitudes, degrees)
    last = np.zeros((1, orders_held, latitudes), np.float32)
    last[0, :2] = rows_np
    starts = np.concatenate([log_np.reshape(n, orders_held, latitudes), last])
    by_order, analysis, synthesis, weights = fourier_exchange(
        field, spectral_weight, forward, n, rows, jnp.asarray(starts), scale, 0
    )

    def to_degrees(table, values):
        values = values.reshape(latitudes, orders_held, 2, half)
        out = dot32("mlj,jmrc->lmrc", table, values).astype(jnp.bfloat16)
        return out.reshape(degrees, rows, half)

    def to_latitudes(table, values):
        values = values.reshape(degrees, orders_held, 2, half)
        out = dot32("mlj,lmrc->jmrc", table, values).astype(jnp.bfloat16)
        return out.reshape(latitudes, rows, half)

    mixed_orders, coeffs = degree_exchange(
        to_degrees(analysis, by_order), spectral_weight, n, mix_scale, 1
    )
    output, grad_by_order = response_exchange(
        to_latitudes(synthesis, mixed_orders),
        field,
        cotangent,
        jnp.asarray(np.ascontiguousarray(inverse_np.T)),
        inverse,
        n,
        3,
    )
    coeff_orders, weight_grad = degree_exchange(
        to_degrees(synthesis, grad_by_order), weights, n, mix_scale, 5, coeffs
    )
    fourier_band = swap(to_latitudes(analysis, coeff_orders), n, False, False, 7)
    field_grad, output, weight_grad = final_field_grad(
        fourier_band,
        cotangent,
        jnp.asarray(np.ascontiguousarray(forward_np.T)),
        output,
        weight_grad,
    )
    return (output, field_grad, weight_grad)


def solution(mesh):
    in_specs = (
        P(("parts", "space"), None, "chan"),
        P("space", None, "chan"),
        P(("parts", "space"), None, "chan"),
    )
    out_specs = (
        P(("parts", "space"), None, "chan"),
        P(("parts", "space"), None, "chan"),
        P(("parts", "space"), None, "chan"),
    )
    return jax.shard_map(local, mesh=mesh, in_specs=in_specs, out_specs=out_specs, check_vma=False)
```

```python
import functools
import math

import jax
import jax.numpy as jnp
import ml_dtypes
import numpy as np
from jax import lax
from jax.experimental import pallas as pl
from jax.experimental.pallas import tpu as pltpu
from jax.sharding import PartitionSpec as P

LIMIT = 2.0**40
SHRINK = 2.0 ** (-40)
LOGSTEP = 40.0 * math.log(2.0)
MESH = pl.DeviceIdType.MESH


def fourier_tables(longitudes, order_list):
    products = (np.asarray(order_list)[:, None] * np.arange(longitudes)[None, :]) % longitudes
    angle = 2.0 * math.pi / longitudes * products
    table = np.stack([np.cos(angle), -np.sin(angle)], axis=1)
    weights = np.where(np.asarray(order_list) == 0, 1.0, 2.0)[:, None, None]
    forward = table.reshape(-1, longitudes).astype(np.float32)
    inverse = (table * weights).reshape(-1, longitudes).astype(np.float32)
    return forward.astype(ml_dtypes.bfloat16), inverse.astype(ml_dtypes.bfloat16)


def latitude_rows(latitudes, longitudes, orders):
    half = latitudes // 2
    north = (np.arange(half) + 0.5) * (math.pi / latitudes)
    cosines = np.concatenate([np.cos(north), -np.cos(north)[::-1]])
    sines = np.concatenate([np.sin(north), np.sin(north)[::-1]])
    order = np.arange(orders)
    gammas = np.array([math.lgamma(m + 0.5) - math.lgamma(m + 1.0) for m in order])
    start = 0.5 * (np.log((2.0 * order + 1.0) / (4.0 * math.pi)) + gammas - 0.5 * math.log(math.pi))
    log_start = start[:, None] + order[:, None] * np.log(sines)[None, :]
    area = latitudes * longitudes
    rows = np.stack([cosines, math.pi**1.5 / math.sqrt(area) * sines])
    return (
        log_start.astype(np.float32),
        rows.astype(np.float32),
        math.sqrt(4.0 * math.pi / area),
    )


def legendre_into(log_start, rows, synthesis_scale, first_order, values, analysis, synthesis):
    held, degrees, latitudes = values.shape
    shape = (held, latitudes)
    order = (lax.broadcasted_iota(jnp.int32, shape, 0) + first_order).astype(jnp.float32)
    cosines = jnp.broadcast_to(rows[0:1, :], shape)
    start = log_start[...]

    def step(at, state):
        previous, before, rescales = state
        degree = at.astype(jnp.float32)
        lower_deg = degree - 1.0
        square = order * order
        upper = jnp.sqrt((4.0 * degree * degree - 1.0) / jnp.maximum(degree * degree - square, 1.0))
        lower = jnp.sqrt(
            jnp.maximum(lower_deg * lower_deg - square, 0.0)
            / jnp.maximum(4.0 * lower_deg * lower_deg - 1.0, 1.0)
        )
        newest = jnp.where(
            degree == order,
            1.0,
            jnp.where(degree > order, upper * (cosines * previous - lower * before), 0.0),
        )
        too_large = jnp.abs(newest) > LIMIT
        newest = jnp.where(too_large, newest * SHRINK, newest)
        previous = jnp.where(too_large, previous * SHRINK, previous)
        rescales = rescales + jnp.where(too_large, 1.0, 0.0)
        values[:, pl.ds(at, 1), :] = (newest * jnp.exp(start + rescales * LOGSTEP))[:, None, :]
        return newest, previous, rescales

    zero = jnp.zeros(shape, jnp.float32)
    lax.fori_loop(0, degrees, step, (zero, zero, zero))
    quadrature = rows[1:2, :]

    def finish(m, carry):
        analysis[m] = (values[m] * quadrature).astype(jnp.bfloat16)
        synthesis[m] = (values[m] * synthesis_scale).astype(jnp.bfloat16)
        return carry

    lax.fori_loop(0, held, finish, 0)


class Exchange:
    def __init__(self, n, held, spread, sparse):
        self.n, self.held, self.spread, self.sparse = n, held, spread, sparse

    def greet(self, chan):
        self.signal(chan)
        self.hear(chan)

    def hear(self, chan):
        pl.semaphore_wait(pltpu.get_barrier_semaphore(), self.n - 1 + (1 if chan else 0))

    def signal(self, chan):
        me = lax.axis_index("space")
        barrier = pltpu.get_barrier_semaphore()
        for k in range(1, self.n):
            pl.semaphore_signal(
                barrier, inc=1, device_id={"space": lax.rem(me + k, self.n)}, device_id_type=MESH
            )
        if chan:
            pl.semaphore_signal(
                barrier, inc=1, device_id={"chan": 1 - lax.axis_index("chan")}, device_id_type=MESH
            )

    def source(self, x, d):
        return x.at[:, d] if self.spread else x.at[pl.ds(d * self.held, self.held)]

    def slot(self, y, s):
        return y.at[pl.ds(s * self.held, self.held)] if self.spread else y.at[:, s]

    def when(self, other, run):
        if self.sparse:
            pl.when(lax.axis_index("space") + other >= self.n - 1)(run)
        else:
            run()

    def copy(self, x, y, k, send_sem, recv_sem, sending):
        me = lax.axis_index("space")
        other = lax.rem(me + k, self.n) if sending else lax.rem(me + self.n - k, self.n)
        return other, pltpu.make_async_remote_copy(
            src_ref=self.source(x, other),
            dst_ref=self.slot(y, me if sending else other),
            send_sem=send_sem.at[k],
            recv_sem=recv_sem.at[k],
            device_id={"space": other},
            device_id_type=MESH,
        )


def send_all(ex, x, y, send_sem, recv_sem):
    for k in range(1, ex.n):
        other, copy = ex.copy(x, y, k, send_sem, recv_sem, True)
        ex.when(other, copy.start)


def wait_sends(ex, x, y, send_sem, recv_sem):
    for k in range(1, ex.n):
        other, copy = ex.copy(x, y, k, send_sem, recv_sem, True)
        ex.when(other, copy.wait_send)


def zero_fill(ex, targets, zero, zero_sem, start):
    me = lax.axis_index("space")
    for k in range(ex.n):
        other = lax.rem(me + ex.n - k, ex.n)

        @pl.when(me + other < ex.n - 1)
        def _():
            for i, y in enumerate(targets):
                copy = pltpu.make_async_copy(zero, ex.slot(y, other), zero_sem.at[i, k])
                copy.start() if start else copy.wait()


def plain_kernel(ex, *refs):
    if ex.sparse:
        x, y, zero, zero_sem, send_sem, recv_sem, own_sem = refs
    else:
        x, y, send_sem, recv_sem, own_sem = refs
    me = lax.axis_index("space")
    ex.greet(False)
    send_all(ex, x, y, send_sem, recv_sem)
    own = pltpu.make_async_copy(ex.source(x, me), ex.slot(y, me), own_sem)
    ex.when(me, own.start)
    if ex.sparse:
        zero[...] = jnp.zeros_like(zero)
        zero_fill(ex, [y], zero, zero_sem, True)
    ex.when(me, own.wait)
    for k in range(1, ex.n):
        other, copy = ex.copy(x, y, k, send_sem, recv_sem, False)
        ex.when(other, copy.wait_recv)
    wait_sends(ex, x, y, send_sem, recv_sem)
    if ex.sparse:
        zero_fill(ex, [y], zero, zero_sem, False)


def any_spec():
    return pl.BlockSpec(memory_space=pl.ANY)


def hbm_spec():
    return pl.BlockSpec(memory_space=pltpu.HBM)


def vmem_spec():
    return pl.BlockSpec(memory_space=pltpu.VMEM)


def params(collective_id, mebibytes=24):
    return pltpu.CompilerParams(
        collective_id=collective_id, has_side_effects=True, vmem_limit_bytes=mebibytes * 2**20
    )


def swap(x, n, spread, sparse, collective_id):
    if spread:
        held, _, rows, width = x.shape
        shape = (n * held, rows, width)
    else:
        total, rows, width = x.shape
        held = total // n
        shape = (held, n, rows, width)
    ex = Exchange(n, held, spread, sparse)
    sems = [
        pltpu.SemaphoreType.DMA((n,)),
        pltpu.SemaphoreType.DMA((n,)),
        pltpu.SemaphoreType.DMA,
    ]
    out = jax.ShapeDtypeStruct(shape, x.dtype)
    scratch = list(sems)
    if sparse:
        zeros = [pltpu.VMEM((held, rows, width), x.dtype), pltpu.SemaphoreType.DMA((1, n))]
        scratch = zeros + scratch
    return pl.pallas_call(
        functools.partial(plain_kernel, ex),
        out_shape=out,
        in_specs=[any_spec()],
        out_specs=any_spec(),
        scratch_shapes=scratch,
        compiler_params=params(collective_id),
        name="exchange",
    )(x)


def flat(block):
    rows = block.shape[0] * block.shape[1]
    return block.astype(jnp.float32).reshape(rows, block.shape[2]).astype(block.dtype)


def unflat(values, n):
    return values.reshape(n, values.shape[0] // n, values.shape[1]).astype(jnp.bfloat16)


def mm(left, right):
    return jnp.dot(left, right, preferred_element_type=jnp.float32)


CHUNK = 4


class Chunked:
    def __init__(self, n, held):
        self.n, self.held = n, held
        self.chunks = held // CHUNK

    def band(self, f, c, d):
        return f.at[pl.ds(c * CHUNK, CHUNK), d]

    def lats(self, y, c, s):
        return y.at[pl.ds(s * self.held + c * CHUNK, CHUNK)]

    def copy(self, x, y, c, k, send_sem, recv_sem, sending, outward):
        me = lax.axis_index("space")
        other = lax.rem(me + k, self.n) if sending else lax.rem(me + self.n - k, self.n)
        here = me if sending else other
        if outward:
            src, dst = self.band(x, c, other), self.lats(y, c, here)
        else:
            src, dst = self.lats(x, c, other), self.band(y, c, here)
        return pltpu.make_async_remote_copy(
            src_ref=src,
            dst_ref=dst,
            send_sem=send_sem.at[c, k],
            recv_sem=recv_sem.at[c, k],
            device_id={"space": other},
            device_id_type=MESH,
        )

    def own(self, x, y, c, sem, outward):
        me = lax.axis_index("space")
        if outward:
            return pltpu.make_async_copy(self.band(x, c, me), self.lats(y, c, me), sem.at[c])
        return pltpu.make_async_copy(self.lats(x, c, me), self.band(y, c, me), sem.at[c])


def fourier_kernel(
    ex,
    synthesis_scale,
    field,
    weight,
    forward_in,
    starts_in,
    y,
    analysis,
    synthesis,
    weights,
    values,
    forward,
    starts,
    held_field,
    bands,
    table_sem,
    load_sem,
    send_sem,
    recv_sem,
    own_sem,
    weight_sem,
):
    n, ch = ex.n, Chunked(ex.n, ex.held)
    me = lax.axis_index("space")
    chan = lax.axis_index("chan")
    half = weight.shape[2]
    loads = [
        pltpu.make_async_copy(
            field.at[pl.ds(c * CHUNK, CHUNK)], held_field.at[pl.ds(c * CHUNK, CHUNK)], load_sem.at[c]
        )
        for c in range(ch.chunks)
    ]
    load_forward = pltpu.make_async_copy(forward_in, forward, table_sem.at[0])
    load_starts = pltpu.make_async_copy(starts_in, starts, table_sem.at[1])
    load_forward.start()
    for load in loads:
        load.start()
    load_starts.start()
    ex.signal(True)
    load_forward.wait()
    keep = pltpu.make_async_copy(
        weight.at[:, pl.ds(pl.multiple_of(chan * half, half), half)], weights.at[0], weight_sem.at[0]
    )
    give = pltpu.make_async_remote_copy(
        src_ref=weight.at[:, pl.ds(pl.multiple_of((1 - chan) * half, half), half)],
        dst_ref=weights.at[1],
        send_sem=weight_sem.at[1],
        recv_sem=weight_sem.at[2],
        device_id={"chan": 1 - chan},
        device_id_type=MESH,
    )
    for c in range(ch.chunks):
        loads[c].wait()

        def pair(i, carry, c=c):
            j = c * CHUNK + 2 * i
            wide = jnp.concatenate([held_field[j], held_field[j + 1]], axis=1)
            out = mm(forward[...], wide)
            bands[j] = unflat(out[:, :half], n)
            bands[j + 1] = unflat(out[:, half:], n)
            return carry

        lax.fori_loop(0, CHUNK // 2, pair, 0)
        if c == 0:
            ex.hear(True)
        for k in range(1, n):
            ch.copy(bands, y, c, k, send_sem, recv_sem, True, True).start()
        ch.own(bands, y, c, own_sem, True).start()
    keep.start()
    give.start()
    load_starts.wait()
    block = n - 1 - order_block(me)
    legendre_into(
        starts.at[block],
        starts.at[n],
        synthesis_scale,
        block * analysis.shape[0],
        values,
        analysis,
        synthesis,
    )
    for c in range(ch.chunks):
        ch.own(bands, y, c, own_sem, True).wait()
        for k in range(1, n):
            ch.copy(bands, y, c, k, send_sem, recv_sem, False, True).wait_recv()
            ch.copy(bands, y, c, k, send_sem, recv_sem, True, True).wait_send()
    keep.wait()
    give.wait()


def fourier_exchange(field, weight, forward, n, rows, starts, scale, collective_id):
    held, longitudes, half = field.shape
    _, orders, latitudes = starts.shape
    degrees = weight.shape[0]
    ex = Exchange(n, held, True, False)
    chunks = held // CHUNK
    table = jax.ShapeDtypeStruct((orders, degrees * n, latitudes), jnp.bfloat16)
    return pl.pallas_call(
        functools.partial(fourier_kernel, ex, scale),
        out_shape=(
            jax.ShapeDtypeStruct((n * held, rows, half), field.dtype),
            table,
            table,
            jax.ShapeDtypeStruct((2, degrees, half, half), field.dtype),
        ),
        in_specs=[hbm_spec()] * 4,
        out_specs=(any_spec(), vmem_spec(), vmem_spec(), any_spec()),
        scratch_shapes=[
            pltpu.VMEM((orders, degrees * n, latitudes), jnp.float32),
            pltpu.VMEM(forward.shape, forward.dtype),
            pltpu.VMEM(starts.shape, starts.dtype),
            pltpu.VMEM((held, longitudes, half), field.dtype),
            pltpu.VMEM((held, n, rows, half), field.dtype),
            pltpu.SemaphoreType.DMA((2,)),
            pltpu.SemaphoreType.DMA((chunks,)),
            pltpu.SemaphoreType.DMA((chunks, n)),
            pltpu.SemaphoreType.DMA((chunks, n)),
            pltpu.SemaphoreType.DMA((chunks,)),
            pltpu.SemaphoreType.DMA((3,)),
        ],
        compiler_params=params(collective_id, 60),
        name="fourier_exchange",
    )(field, weight, forward, starts)


TILE = 128


def response_kernel(
    ex,
    grid,
    field,
    cotangent,
    inverse_t,
    inverse,
    output,
    y,
    held_field,
    held_cot,
    arrived,
    slopes,
    bands,
    load_sem,
    in_send,
    in_recv,
    in_own,
    out_send,
    out_recv,
    out_own,
    store_sem,
):
    n, ch = ex.n, Chunked(ex.n, ex.held)
    half = field.shape[2]
    tiles = field.shape[1] // TILE

    def part(ref, c):
        return ref.at[pl.ds(c * CHUNK, CHUNK)]

    def loads(c):
        return (
            pltpu.make_async_copy(part(field, c), part(held_field, c), load_sem.at[0, c]),
            pltpu.make_async_copy(part(cotangent, c), part(held_cot, c), load_sem.at[1, c]),
        )

    def store(c):
        return pltpu.make_async_copy(part(held_field, c), part(output, c), store_sem.at[c])

    for c in range(ch.chunks):
        for load in loads(c):
            load.start()
    ex.greet(False)
    for c in range(ch.chunks):
        for k in range(1, n):
            ch.copy(grid, arrived, c, k, in_send, in_recv, True, False).start()
        ch.own(grid, arrived, c, in_own, False).start()
    for c in range(ch.chunks):
        for load in loads(c):
            load.wait()
        ch.own(grid, arrived, c, in_own, False).wait()
        for k in range(1, n):
            ch.copy(grid, arrived, c, k, in_send, in_recv, False, False).wait_recv()

        def pair(i, carry, c=c):
            j = c * CHUNK + 2 * i
            wide = jnp.concatenate([flat(arrived[j]), flat(arrived[j + 1])], axis=1)

            def tile(t, inner):
                at = pl.ds(pl.multiple_of(t * TILE, TILE), TILE)
                response = mm(inverse_t[at, :], wide)
                cdf = 0.5 * (1.0 + lax.erf(response * (1.0 / math.sqrt(2.0))))
                density = jnp.exp(-0.5 * response * response) * (1.0 / math.sqrt(2.0 * math.pi))
                gain = response * cdf
                slope = cdf + response * density
                for side in range(2):
                    lanes = slice(side * half, (side + 1) * half)
                    base = held_field[j + side, at, :].astype(jnp.float32)
                    held_field[j + side, at, :] = (base + gain[:, lanes]).astype(jnp.bfloat16)
                    cot = held_cot[j + side, at, :].astype(jnp.float32)
                    slopes[at, lanes] = (cot * slope[:, lanes]).astype(jnp.bfloat16)
                return inner

            lax.fori_loop(0, tiles, tile, 0)
            out = mm(inverse[...], slopes[...])
            bands[j] = unflat(out[:, :half], n)
            bands[j + 1] = unflat(out[:, half:], n)
            return carry

        lax.fori_loop(0, CHUNK // 2, pair, 0)
        for k in range(1, n):
            ch.copy(bands, y, c, k, out_send, out_recv, True, True).start()
        ch.own(bands, y, c, out_own, True).start()
        store(c).start()
    for c in range(ch.chunks):
        ch.own(bands, y, c, out_own, True).wait()
        store(c).wait()
        for k in range(1, n):
            ch.copy(bands, y, c, k, out_send, out_recv, False, True).wait_recv()
            ch.copy(bands, y, c, k, out_send, out_recv, True, True).wait_send()
            ch.copy(grid, arrived, c, k, in_send, in_recv, True, False).wait_send()


def response_exchange(grid, field, cotangent, inverse_t, inverse, n, collective_id):
    held, longitudes, half = field.shape
    rows = grid.shape[1]
    chunks = held // CHUNK
    ex = Exchange(n, held, True, False)
    return pl.pallas_call(
        functools.partial(response_kernel, ex),
        out_shape=(
            jax.ShapeDtypeStruct(field.shape, field.dtype),
            jax.ShapeDtypeStruct((n * held, rows, half), field.dtype),
        ),
        in_specs=[any_spec(), hbm_spec(), hbm_spec()] + [vmem_spec()] * 2,
        out_specs=(any_spec(), any_spec()),
        scratch_shapes=[
            pltpu.VMEM((held, longitudes, half), field.dtype),
            pltpu.VMEM((held, longitudes, half), field.dtype),
            pltpu.VMEM((held, n, rows, half), field.dtype),
            pltpu.VMEM((longitudes, 2 * half), field.dtype),
            pltpu.VMEM((held, n, rows, half), field.dtype),
            pltpu.SemaphoreType.DMA((2, chunks)),
            pltpu.SemaphoreType.DMA((chunks, n)),
            pltpu.SemaphoreType.DMA((chunks, n)),
            pltpu.SemaphoreType.DMA((chunks,)),
            pltpu.SemaphoreType.DMA((chunks, n)),
            pltpu.SemaphoreType.DMA((chunks, n)),
            pltpu.SemaphoreType.DMA((chunks,)),
            pltpu.SemaphoreType.DMA((chunks,)),
        ],
        compiler_params=params(collective_id, 60),
        name="response_exchange",
    )(grid, field, cotangent, inverse_t, inverse)


def field_grad_kernel(
    band, cotangent, forward_t, output, weight_grad, out, output_out, weight_out, sem
):
    half = band.shape[-1]
    passing = [
        pltpu.make_async_copy(output, output_out, sem.at[0]),
        pltpu.make_async_copy(weight_grad, weight_out, sem.at[1]),
    ]

    @pl.when(pl.program_id(0) == 0)
    def _():
        for copy in passing:
            copy.start()

    for i in range(0, band.shape[0], 2):
        wide = jnp.concatenate([flat(band[i]), flat(band[i + 1])], axis=1)
        total = mm(forward_t[...], wide)
        for side in range(2):
            part = total[:, side * half : (side + 1) * half]
            out[i + side] = (cotangent[i + side].astype(jnp.float32) + part).astype(out.dtype)

    @pl.when(pl.program_id(0) == pl.num_programs(0) - 1)
    def _():
        for copy in passing:
            copy.wait()


def final_field_grad(band, cotangent, forward_t, output, weight_grad):
    held, n, rows, half = band.shape
    longitudes = cotangent.shape[1]
    lat = pl.BlockSpec((2, longitudes, half), lambda i: (i, 0, 0))
    return pl.pallas_call(
        field_grad_kernel,
        grid=(held // 2,),
        out_shape=tuple(
            jax.ShapeDtypeStruct(like.shape, like.dtype) for like in (cotangent, output, weight_grad)
        ),
        in_specs=[
            pl.BlockSpec((2, n, rows, half), lambda i: (i, 0, 0, 0)),
            lat,
            pl.BlockSpec(forward_t.shape, lambda i: (0, 0)),
            any_spec(),
            any_spec(),
        ],
        out_specs=(lat, any_spec(), any_spec()),
        scratch_shapes=[pltpu.SemaphoreType.DMA((2,))],
        compiler_params=pltpu.CompilerParams(vmem_limit_bytes=24 * 2**20),
        name="field_grad",
    )(band, cotangent, forward_t, output, weight_grad)


def order_block(s):
    return s + ((s // 2) % 2) * (1 - 2 * (s % 2))


def holds(n, orders_at, degrees_at):
    return order_block(orders_at) + degrees_at >= n - 1


def degree_kernel(n, backward, scale, *refs):
    if backward:
        x, weights, coeffs, y, weight_grad, blocks = refs[:6]
    else:
        x, weights, y, blocks = refs[:4]
    mixed, zero, zero_sem, send1, recv1, own1, fsend, frecv, send2, recv2, own2 = refs[-11:]
    me = lax.axis_index("space")
    chan = lax.axis_index("chan")
    held, half = blocks.shape[1], blocks.shape[-1]
    mine = pl.ds(pl.multiple_of(chan * half, half), half)
    theirs = pl.ds(pl.multiple_of((1 - chan) * half, half), half)
    Exchange(n, held, False, True).greet(True)

    def ahead(k):
        return lax.rem(me + k, n)

    def behind(k):
        return lax.rem(me + n - k, n)

    def rows_of(ref, d):
        return ref.at[pl.ds(d * held, held)]

    def coming(k, sending):
        return pltpu.make_async_remote_copy(
            src_ref=rows_of(x, ahead(k)),
            dst_ref=blocks.at[0, :, me if sending else behind(k)],
            send_sem=send1.at[k],
            recv_sem=recv1.at[k],
            device_id={"space": ahead(k) if sending else behind(k)},
            device_id_type=MESH,
        )

    def across(k):
        return pltpu.make_async_remote_copy(
            src_ref=blocks.at[0, :, behind(k)],
            dst_ref=blocks.at[1, :, behind(k)],
            send_sem=fsend.at[k],
            recv_sem=frecv.at[k],
            device_id={"chan": 1 - chan},
            device_id_type=MESH,
        )

    def going(k, sending):
        return pltpu.make_async_remote_copy(
            src_ref=mixed.at[:, behind(k)],
            dst_ref=rows_of(y, me if sending else ahead(k)),
            send_sem=send2.at[k],
            recv_sem=recv2.at[k],
            device_id={"space": behind(k) if sending else ahead(k)},
            device_id_type=MESH,
        )

    def start_coming(k, carry):
        pl.when(holds(n, me, ahead(k)))(lambda: coming(k, True).start())
        return carry

    lax.fori_loop(1, n, start_coming, 0)
    own_in = pltpu.make_async_copy(rows_of(x, me), blocks.at[0, :, me], own1)
    own_out = pltpu.make_async_copy(mixed.at[:, me], rows_of(y, me), own2)
    zero[...] = jnp.zeros_like(zero)

    def zeros_of(k):
        return pltpu.make_async_copy(zero, rows_of(y, ahead(k)), zero_sem.at[k])

    def fill(k, carry):
        other = behind(k)

        @pl.when(jnp.logical_not(holds(n, other, me)))
        def _():
            for side in range(2):
                for at in range(held):
                    blocks[side, at, other] = jnp.zeros(blocks.shape[3:], blocks.dtype)

        pl.when(jnp.logical_not(holds(n, me, ahead(k))))(lambda: zeros_of(k).start())
        return carry

    def mix(other):
        for at in range(held):
            wide = jnp.concatenate([blocks[0, at, other], blocks[1, at, other]], axis=1)
            if backward:
                weight = jnp.concatenate([weights[0, at], weights[1, at]], axis=1)
                total = lax.dot_general(
                    wide, weight, (((1,), (1,)), ((), ())), preferred_element_type=jnp.float32
                )
            else:
                weight = jnp.concatenate([weights[at, mine, :], weights[at, theirs, :]], axis=0)
                total = mm(wide, weight)
            mixed[at, other] = (total * scale).astype(mixed.dtype)

    has_own = holds(n, me, me)

    @pl.when(has_own)
    def _():
        own_in.start()
        own_in.wait()
        across(0).start()

    lax.fori_loop(0, n, fill, 0)

    def settle(k):
        across(k).wait_recv()
        mix(behind(k))
        going(k, True).start()

    def turn(k, carry):
        @pl.when(holds(n, behind(k), me))
        def _():
            coming(k, False).wait_recv()
            across(k).start()

        @pl.when(jnp.logical_and(k > 1, holds(n, behind(k - 1), me)))
        def _():
            settle(k - 1)

        return carry

    lax.fori_loop(1, n, turn, 0)
    pl.when(holds(n, behind(n - 1), me))(lambda: settle(n - 1))

    @pl.when(has_own)
    def _():
        across(0).wait_recv()
        mix(me)
        own_out.start()

    if backward:

        def products(at, carry):
            grad = flat(blocks[0, at])
            for side, lines in ((0, mine), (1, theirs)):
                part = lax.dot_general(
                    flat(coeffs[side, at]),
                    grad,
                    (((0,), (0,)), ((), ())),
                    preferred_element_type=jnp.float32,
                )
                weight_grad[at, lines, :] = (part * scale).astype(weight_grad.dtype)
            return carry

        lax.fori_loop(0, held, products, 0)

    @pl.when(has_own)
    def _():
        own_out.wait()
        across(0).wait_send()

    def finish(k, carry):
        @pl.when(holds(n, behind(k), me))
        def _():
            across(k).wait_send()
            going(k, True).wait_send()

        @pl.when(holds(n, me, ahead(k)))
        def _():
            coming(k, True).wait_send()
            going(k, False).wait_recv()

        return carry

    lax.fori_loop(1, n, finish, 0)

    def filled(k, carry):
        pl.when(jnp.logical_not(holds(n, me, ahead(k))))(lambda: zeros_of(k).wait())
        return carry

    lax.fori_loop(0, n, filled, 0)


def degree_exchange(x, weights, n, scale, collective_id, coeffs=None):
    total, rows, half = x.shape
    held = total // n
    backward = coeffs is not None
    block = jax.ShapeDtypeStruct((2, held, n, rows, half), x.dtype)
    shapes = [jax.ShapeDtypeStruct(x.shape, x.dtype)]
    specs = [any_spec(), vmem_spec()]
    scratch = []
    if backward:
        shapes.append(jax.ShapeDtypeStruct((held, 2 * half, half), x.dtype))
        scratch.append(pltpu.VMEM(block.shape, x.dtype))
    else:
        shapes.append(block)
    dma = pltpu.SemaphoreType.DMA
    return pl.pallas_call(
        functools.partial(degree_kernel, n, backward, scale),
        out_shape=tuple(shapes),
        in_specs=[any_spec()] + [vmem_spec()] * (2 if backward else 1),
        out_specs=tuple(specs),
        scratch_shapes=scratch
        + [
            pltpu.VMEM((held, n, rows, half), x.dtype),
            pltpu.VMEM((held, rows, half), x.dtype),
            dma((n,)),
            dma((n,)),
            dma((n,)),
            dma,
            dma((n,)),
            dma((n,)),
            dma((n,)),
            dma((n,)),
            dma,
        ],
        compiler_params=params(collective_id),
        name="degree_exchange",
    )(*([x, weights] + ([coeffs] if backward else [])))


def dot32(formula, left, right):
    return jnp.einsum(formula, left, right, preferred_element_type=jnp.float32)


def local(field, spectral_weight, cotangent):
    n = lax.axis_size("space")
    held, longitudes, half = field.shape
    degrees_held, channels, _ = spectral_weight.shape
    latitudes = held * n
    degrees = degrees_held * n
    orders_held = degrees_held
    rows = 2 * orders_held
    mix_scale = 1.0 / math.sqrt(channels)
    chan = lax.axis_index("chan")
    held_blocks = [n - 1 - order_block(s) for s in range(n)]
    order_list = np.arange(degrees).reshape(n, orders_held)[held_blocks].reshape(-1)
    forward_np, inverse_np = fourier_tables(longitudes, order_list)
    forward, inverse = jnp.asarray(forward_np), jnp.asarray(inverse_np)
    log_np, rows_np, scale = latitude_rows(latitudes, longitudes, degrees)
    last = np.zeros((1, orders_held, latitudes), np.float32)
    last[0, :2] = rows_np
    starts = np.concatenate([log_np.reshape(n, orders_held, latitudes), last])
    by_order, analysis, synthesis, weights = fourier_exchange(
        field, spectral_weight, forward, n, rows, jnp.asarray(starts), scale, 0
    )

    def to_degrees(table, values):
        values = values.reshape(latitudes, orders_held, 2, half)
        out = dot32("mlj,jmrc->lmrc", table, values).astype(jnp.bfloat16)
        return out.reshape(degrees, rows, half)

    def to_latitudes(table, values):
        values = values.reshape(degrees, orders_held, 2, half)
        out = dot32("mlj,lmrc->jmrc", table, values).astype(jnp.bfloat16)
        return out.reshape(latitudes, rows, half)

    mixed_orders, coeffs = degree_exchange(
        to_degrees(analysis, by_order), spectral_weight, n, mix_scale, 1
    )
    output, grad_by_order = response_exchange(
        to_latitudes(synthesis, mixed_orders),
        field,
        cotangent,
        jnp.asarray(np.ascontiguousarray(inverse_np.T)),
        inverse,
        n,
        3,
    )
    coeff_orders, weight_grad = degree_exchange(
        to_degrees(synthesis, grad_by_order), weights, n, mix_scale, 5, coeffs
    )
    fourier_band = swap(to_latitudes(analysis, coeff_orders), n, False, False, 7)
    field_grad, output, weight_grad = final_field_grad(
        fourier_band,
        cotangent,
        jnp.asarray(np.ascontiguousarray(forward_np.T)),
        output,
        weight_grad,
    )
    return (output, field_grad, weight_grad)


def solution(mesh):
    in_specs = (
        P(("parts", "space"), None, "chan"),
        P("space", None, "chan"),
        P(("parts", "space"), None, "chan"),
    )
    out_specs = (
        P(("parts", "space"), None, "chan"),
        P(("parts", "space"), None, "chan"),
        P(("parts", "space"), None, "chan"),
    )
    return jax.shard_map(local, mesh=mesh, in_specs=in_specs, out_specs=out_specs, check_vma=False)
```

```python
import functools
import math

import jax
import jax.numpy as jnp
import ml_dtypes
import numpy as np
from jax import lax
from jax.experimental import pallas as pl
from jax.experimental.pallas import tpu as pltpu
from jax.sharding import PartitionSpec as P

LIMIT = 2.0**40
SHRINK = 2.0 ** (-40)
LOGSTEP = 40.0 * math.log(2.0)
MESH = pl.DeviceIdType.MESH


def fourier_tables(longitudes, order_list):
    products = (np.asarray(order_list)[:, None] * np.arange(longitudes)[None, :]) % longitudes
    angle = 2.0 * math.pi / longitudes * products
    table = np.stack([np.cos(angle), -np.sin(angle)], axis=1)
    weights = np.where(np.asarray(order_list) == 0, 1.0, 2.0)[:, None, None]
    forward = table.reshape(-1, longitudes).astype(np.float32)
    inverse = (table * weights).reshape(-1, longitudes).astype(np.float32)
    return forward.astype(ml_dtypes.bfloat16), inverse.astype(ml_dtypes.bfloat16)


def latitude_rows(latitudes, longitudes, orders):
    half = latitudes // 2
    north = (np.arange(half) + 0.5) * (math.pi / latitudes)
    cosines = np.concatenate([np.cos(north), -np.cos(north)[::-1]])
    sines = np.concatenate([np.sin(north), np.sin(north)[::-1]])
    order = np.arange(orders)
    gammas = np.array([math.lgamma(m + 0.5) - math.lgamma(m + 1.0) for m in order])
    start = 0.5 * (np.log((2.0 * order + 1.0) / (4.0 * math.pi)) + gammas - 0.5 * math.log(math.pi))
    log_start = start[:, None] + order[:, None] * np.log(sines)[None, :]
    area = latitudes * longitudes
    rows = np.stack([cosines, math.pi**1.5 / math.sqrt(area) * sines])
    return (
        log_start.astype(np.float32),
        rows.astype(np.float32),
        math.sqrt(4.0 * math.pi / area),
    )


def legendre_into(log_start, rows, synthesis_scale, first_order, values, analysis, synthesis):
    held, degrees, latitudes = values.shape
    shape = (held, latitudes)
    order = (lax.broadcasted_iota(jnp.int32, shape, 0) + first_order).astype(jnp.float32)
    cosines = jnp.broadcast_to(rows[0:1, :], shape)
    start = log_start[...]

    def step(at, state):
        previous, before, rescales = state
        degree = at.astype(jnp.float32)
        lower_deg = degree - 1.0
        square = order * order
        upper = jnp.sqrt((4.0 * degree * degree - 1.0) / jnp.maximum(degree * degree - square, 1.0))
        lower = jnp.sqrt(
            jnp.maximum(lower_deg * lower_deg - square, 0.0)
            / jnp.maximum(4.0 * lower_deg * lower_deg - 1.0, 1.0)
        )
        newest = jnp.where(
            degree == order,
            1.0,
            jnp.where(degree > order, upper * (cosines * previous - lower * before), 0.0),
        )
        too_large = jnp.abs(newest) > LIMIT
        newest = jnp.where(too_large, newest * SHRINK, newest)
        previous = jnp.where(too_large, previous * SHRINK, previous)
        rescales = rescales + jnp.where(too_large, 1.0, 0.0)
        values[:, pl.ds(at, 1), :] = (newest * jnp.exp(start + rescales * LOGSTEP))[:, None, :]
        return newest, previous, rescales

    zero = jnp.zeros(shape, jnp.float32)
    lax.fori_loop(0, degrees, step, (zero, zero, zero))
    quadrature = rows[1:2, :]

    def finish(m, carry):
        analysis[m] = (values[m] * quadrature).astype(jnp.bfloat16)
        synthesis[m] = (values[m] * synthesis_scale).astype(jnp.bfloat16)
        return carry

    lax.fori_loop(0, held, finish, 0)


class Exchange:
    def __init__(self, n, held, spread, sparse):
        self.n, self.held, self.spread, self.sparse = n, held, spread, sparse

    def greet(self, chan):
        self.signal(chan)
        self.hear(chan)

    def hear(self, chan):
        pl.semaphore_wait(pltpu.get_barrier_semaphore(), self.n - 1 + (1 if chan else 0))

    def signal(self, chan):
        me = lax.axis_index("space")
        barrier = pltpu.get_barrier_semaphore()
        for k in range(1, self.n):
            pl.semaphore_signal(
                barrier, inc=1, device_id={"space": lax.rem(me + k, self.n)}, device_id_type=MESH
            )
        if chan:
            pl.semaphore_signal(
                barrier, inc=1, device_id={"chan": 1 - lax.axis_index("chan")}, device_id_type=MESH
            )

    def source(self, x, d):
        return x.at[:, d] if self.spread else x.at[pl.ds(d * self.held, self.held)]

    def slot(self, y, s):
        return y.at[pl.ds(s * self.held, self.held)] if self.spread else y.at[:, s]

    def when(self, other, run):
        if self.sparse:
            pl.when(lax.axis_index("space") + other >= self.n - 1)(run)
        else:
            run()

    def copy(self, x, y, k, send_sem, recv_sem, sending):
        me = lax.axis_index("space")
        other = lax.rem(me + k, self.n) if sending else lax.rem(me + self.n - k, self.n)
        return other, pltpu.make_async_remote_copy(
            src_ref=self.source(x, other),
            dst_ref=self.slot(y, me if sending else other),
            send_sem=send_sem.at[k],
            recv_sem=recv_sem.at[k],
            device_id={"space": other},
            device_id_type=MESH,
        )


def send_all(ex, x, y, send_sem, recv_sem):
    for k in range(1, ex.n):
        other, copy = ex.copy(x, y, k, send_sem, recv_sem, True)
        ex.when(other, copy.start)


def wait_sends(ex, x, y, send_sem, recv_sem):
    for k in range(1, ex.n):
        other, copy = ex.copy(x, y, k, send_sem, recv_sem, True)
        ex.when(other, copy.wait_send)


def zero_fill(ex, targets, zero, zero_sem, start):
    me = lax.axis_index("space")
    for k in range(ex.n):
        other = lax.rem(me + ex.n - k, ex.n)

        @pl.when(me + other < ex.n - 1)
        def _():
            for i, y in enumerate(targets):
                copy = pltpu.make_async_copy(zero, ex.slot(y, other), zero_sem.at[i, k])
                copy.start() if start else copy.wait()


def plain_kernel(ex, *refs):
    if ex.sparse:
        x, y, zero, zero_sem, send_sem, recv_sem, own_sem = refs
    else:
        x, y, send_sem, recv_sem, own_sem = refs
    me = lax.axis_index("space")
    ex.greet(False)
    send_all(ex, x, y, send_sem, recv_sem)
    own = pltpu.make_async_copy(ex.source(x, me), ex.slot(y, me), own_sem)
    ex.when(me, own.start)
    if ex.sparse:
        zero[...] = jnp.zeros_like(zero)
        zero_fill(ex, [y], zero, zero_sem, True)
    ex.when(me, own.wait)
    for k in range(1, ex.n):
        other, copy = ex.copy(x, y, k, send_sem, recv_sem, False)
        ex.when(other, copy.wait_recv)
    wait_sends(ex, x, y, send_sem, recv_sem)
    if ex.sparse:
        zero_fill(ex, [y], zero, zero_sem, False)


def any_spec():
    return pl.BlockSpec(memory_space=pl.ANY)


def hbm_spec():
    return pl.BlockSpec(memory_space=pltpu.HBM)


def vmem_spec():
    return pl.BlockSpec(memory_space=pltpu.VMEM)


def params(collective_id, mebibytes=24):
    return pltpu.CompilerParams(
        collective_id=collective_id, has_side_effects=True, vmem_limit_bytes=mebibytes * 2**20
    )


def swap(x, n, spread, sparse, collective_id):
    if spread:
        held, _, rows, width = x.shape
        shape = (n * held, rows, width)
    else:
        total, rows, width = x.shape
        held = total // n
        shape = (held, n, rows, width)
    ex = Exchange(n, held, spread, sparse)
    sems = [
        pltpu.SemaphoreType.DMA((n,)),
        pltpu.SemaphoreType.DMA((n,)),
        pltpu.SemaphoreType.DMA,
    ]
    out = jax.ShapeDtypeStruct(shape, x.dtype)
    scratch = list(sems)
    if sparse:
        zeros = [pltpu.VMEM((held, rows, width), x.dtype), pltpu.SemaphoreType.DMA((1, n))]
        scratch = zeros + scratch
    return pl.pallas_call(
        functools.partial(plain_kernel, ex),
        out_shape=out,
        in_specs=[any_spec()],
        out_specs=any_spec(),
        scratch_shapes=scratch,
        compiler_params=params(collective_id),
        name="exchange",
    )(x)


def flat(block):
    rows = block.shape[0] * block.shape[1]
    return block.astype(jnp.float32).reshape(rows, block.shape[2]).astype(block.dtype)


def unflat(values, n):
    return values.reshape(n, values.shape[0] // n, values.shape[1]).astype(jnp.bfloat16)


def mm(left, right):
    return jnp.dot(left, right, preferred_element_type=jnp.float32)


CHUNK = 4


class Chunked:
    def __init__(self, n, held):
        self.n, self.held = n, held
        self.chunks = held // CHUNK

    def band(self, f, c, d):
        return f.at[pl.ds(c * CHUNK, CHUNK), d]

    def lats(self, y, c, s):
        return y.at[pl.ds(s * self.held + c * CHUNK, CHUNK)]

    def copy(self, x, y, c, k, send_sem, recv_sem, sending, outward):
        me = lax.axis_index("space")
        other = lax.rem(me + k, self.n) if sending else lax.rem(me + self.n - k, self.n)
        here = me if sending else other
        if outward:
            src, dst = self.band(x, c, other), self.lats(y, c, here)
        else:
            src, dst = self.lats(x, c, other), self.band(y, c, here)
        return pltpu.make_async_remote_copy(
            src_ref=src,
            dst_ref=dst,
            send_sem=send_sem.at[c, k],
            recv_sem=recv_sem.at[c, k],
            device_id={"space": other},
            device_id_type=MESH,
        )

    def own(self, x, y, c, sem, outward):
        me = lax.axis_index("space")
        if outward:
            return pltpu.make_async_copy(self.band(x, c, me), self.lats(y, c, me), sem.at[c])
        return pltpu.make_async_copy(self.lats(x, c, me), self.band(y, c, me), sem.at[c])


def fourier_kernel(
    ex,
    synthesis_scale,
    field,
    weight,
    forward_in,
    starts_in,
    y,
    analysis,
    synthesis,
    weights,
    values,
    forward,
    starts,
    held_field,
    bands,
    table_sem,
    load_sem,
    send_sem,
    recv_sem,
    own_sem,
    weight_sem,
):
    n, ch = ex.n, Chunked(ex.n, ex.held)
    me = lax.axis_index("space")
    chan = lax.axis_index("chan")
    half = weight.shape[2]
    loads = [
        pltpu.make_async_copy(
            field.at[pl.ds(c * CHUNK, CHUNK)], held_field.at[pl.ds(c * CHUNK, CHUNK)], load_sem.at[c]
        )
        for c in range(ch.chunks)
    ]
    load_forward = pltpu.make_async_copy(forward_in, forward, table_sem.at[0])
    load_starts = pltpu.make_async_copy(starts_in, starts, table_sem.at[1])
    load_forward.start()
    for load in loads:
        load.start()
    load_starts.start()
    ex.signal(True)
    load_forward.wait()
    keep = pltpu.make_async_copy(
        weight.at[:, pl.ds(pl.multiple_of(chan * half, half), half)], weights.at[0], weight_sem.at[0]
    )
    give = pltpu.make_async_remote_copy(
        src_ref=weight.at[:, pl.ds(pl.multiple_of((1 - chan) * half, half), half)],
        dst_ref=weights.at[1],
        send_sem=weight_sem.at[1],
        recv_sem=weight_sem.at[2],
        device_id={"chan": 1 - chan},
        device_id_type=MESH,
    )
    for c in range(ch.chunks):
        loads[c].wait()

        def pair(i, carry, c=c):
            j = c * CHUNK + 2 * i
            wide = jnp.concatenate([held_field[j], held_field[j + 1]], axis=1)
            out = mm(forward[...], wide)
            bands[j] = unflat(out[:, :half], n)
            bands[j + 1] = unflat(out[:, half:], n)
            return carry

        lax.fori_loop(0, CHUNK // 2, pair, 0)
        if c == 0:
            ex.hear(True)
        for k in range(1, n):
            ch.copy(bands, y, c, k, send_sem, recv_sem, True, True).start()
        ch.own(bands, y, c, own_sem, True).start()
    keep.start()
    give.start()
    load_starts.wait()
    block = n - 1 - order_block(me)
    legendre_into(
        starts.at[block],
        starts.at[n],
        synthesis_scale,
        block * analysis.shape[0],
        values,
        analysis,
        synthesis,
    )
    for c in range(ch.chunks):
        ch.own(bands, y, c, own_sem, True).wait()
        for k in range(1, n):
            ch.copy(bands, y, c, k, send_sem, recv_sem, False, True).wait_recv()
            ch.copy(bands, y, c, k, send_sem, recv_sem, True, True).wait_send()
    keep.wait()
    give.wait()


def fourier_exchange(field, weight, forward, n, rows, starts, scale, collective_id):
    held, longitudes, half = field.shape
    _, orders, latitudes = starts.shape
    degrees = weight.shape[0]
    ex = Exchange(n, held, True, False)
    chunks = held // CHUNK
    table = jax.ShapeDtypeStruct((orders, degrees * n, latitudes), jnp.bfloat16)
    return pl.pallas_call(
        functools.partial(fourier_kernel, ex, scale),
        out_shape=(
            jax.ShapeDtypeStruct((n * held, rows, half), field.dtype),
            table,
            table,
            jax.ShapeDtypeStruct((2, degrees, half, half), field.dtype),
        ),
        in_specs=[hbm_spec()] * 4,
        out_specs=(any_spec(), vmem_spec(), vmem_spec(), any_spec()),
        scratch_shapes=[
            pltpu.VMEM((orders, degrees * n, latitudes), jnp.float32),
            pltpu.VMEM(forward.shape, forward.dtype),
            pltpu.VMEM(starts.shape, starts.dtype),
            pltpu.VMEM((held, longitudes, half), field.dtype),
            pltpu.VMEM((held, n, rows, half), field.dtype),
            pltpu.SemaphoreType.DMA((2,)),
            pltpu.SemaphoreType.DMA((chunks,)),
            pltpu.SemaphoreType.DMA((chunks, n)),
            pltpu.SemaphoreType.DMA((chunks, n)),
            pltpu.SemaphoreType.DMA((chunks,)),
            pltpu.SemaphoreType.DMA((3,)),
        ],
        compiler_params=params(collective_id),
        name="fourier_exchange",
    )(field, weight, forward, starts)


TILE = 128


def response_kernel(
    ex,
    grid,
    field,
    cotangent,
    inverse_t,
    inverse,
    output,
    y,
    held_field,
    held_cot,
    arrived,
    slopes,
    bands,
    load_sem,
    in_send,
    in_recv,
    in_own,
    out_send,
    out_recv,
    out_own,
    store_sem,
):
    n, ch = ex.n, Chunked(ex.n, ex.held)
    half = field.shape[2]
    tiles = field.shape[1] // TILE

    def part(ref, c):
        return ref.at[pl.ds(c * CHUNK, CHUNK)]

    def loads(c):
        return (
            pltpu.make_async_copy(part(field, c), part(held_field, c), load_sem.at[0, c]),
            pltpu.make_async_copy(part(cotangent, c), part(held_cot, c), load_sem.at[1, c]),
        )

    def store(c):
        return pltpu.make_async_copy(part(held_field, c), part(output, c), store_sem.at[c])

    for c in range(ch.chunks):
        for load in loads(c):
            load.start()
    ex.greet(False)
    for c in range(ch.chunks):
        for k in range(1, n):
            ch.copy(grid, arrived, c, k, in_send, in_recv, True, False).start()
        ch.own(grid, arrived, c, in_own, False).start()
    for c in range(ch.chunks):
        for load in loads(c):
            load.wait()
        ch.own(grid, arrived, c, in_own, False).wait()
        for k in range(1, n):
            ch.copy(grid, arrived, c, k, in_send, in_recv, False, False).wait_recv()

        def pair(i, carry, c=c):
            j = c * CHUNK + 2 * i
            wide = jnp.concatenate([flat(arrived[j]), flat(arrived[j + 1])], axis=1)

            def tile(t, inner):
                at = pl.ds(pl.multiple_of(t * TILE, TILE), TILE)
                response = mm(inverse_t[at, :], wide)
                cdf = 0.5 * (1.0 + lax.erf(response * (1.0 / math.sqrt(2.0))))
                density = jnp.exp(-0.5 * response * response) * (1.0 / math.sqrt(2.0 * math.pi))
                gain = response * cdf
                slope = cdf + response * density
                for side in range(2):
                    lanes = slice(side * half, (side + 1) * half)
                    base = held_field[j + side, at, :].astype(jnp.float32)
                    held_field[j + side, at, :] = (base + gain[:, lanes]).astype(jnp.bfloat16)
                    cot = held_cot[j + side, at, :].astype(jnp.float32)
                    slopes[at, lanes] = (cot * slope[:, lanes]).astype(jnp.bfloat16)
                return inner

            lax.fori_loop(0, tiles, tile, 0)
            out = mm(inverse[...], slopes[...])
            bands[j] = unflat(out[:, :half], n)
            bands[j + 1] = unflat(out[:, half:], n)
            return carry

        lax.fori_loop(0, CHUNK // 2, pair, 0)
        for k in range(1, n):
            ch.copy(bands, y, c, k, out_send, out_recv, True, True).start()
        ch.own(bands, y, c, out_own, True).start()
        store(c).start()
    for c in range(ch.chunks):
        ch.own(bands, y, c, out_own, True).wait()
        store(c).wait()
        for k in range(1, n):
            ch.copy(bands, y, c, k, out_send, out_recv, False, True).wait_recv()
            ch.copy(bands, y, c, k, out_send, out_recv, True, True).wait_send()
            ch.copy(grid, arrived, c, k, in_send, in_recv, True, False).wait_send()


def response_exchange(grid, field, cotangent, inverse_t, inverse, n, collective_id):
    held, longitudes, half = field.shape
    rows = grid.shape[1]
    chunks = held // CHUNK
    ex = Exchange(n, held, True, False)
    return pl.pallas_call(
        functools.partial(response_kernel, ex),
        out_shape=(
            jax.ShapeDtypeStruct(field.shape, field.dtype),
            jax.ShapeDtypeStruct((n * held, rows, half), field.dtype),
        ),
        in_specs=[any_spec(), hbm_spec(), hbm_spec()] + [vmem_spec()] * 2,
        out_specs=(any_spec(), any_spec()),
        scratch_shapes=[
            pltpu.VMEM((held, longitudes, half), field.dtype),
            pltpu.VMEM((held, longitudes, half), field.dtype),
            pltpu.VMEM((held, n, rows, half), field.dtype),
            pltpu.VMEM((longitudes, 2 * half), field.dtype),
            pltpu.VMEM((held, n, rows, half), field.dtype),
            pltpu.SemaphoreType.DMA((2, chunks)),
            pltpu.SemaphoreType.DMA((chunks, n)),
            pltpu.SemaphoreType.DMA((chunks, n)),
            pltpu.SemaphoreType.DMA((chunks,)),
            pltpu.SemaphoreType.DMA((chunks, n)),
            pltpu.SemaphoreType.DMA((chunks, n)),
            pltpu.SemaphoreType.DMA((chunks,)),
            pltpu.SemaphoreType.DMA((chunks,)),
        ],
        compiler_params=params(collective_id),
        name="response_exchange",
    )(grid, field, cotangent, inverse_t, inverse)


def field_grad_kernel(
    band, cotangent, forward_t, output, weight_grad, out, output_out, weight_out, sem
):
    half = band.shape[-1]
    passing = [
        pltpu.make_async_copy(output, output_out, sem.at[0]),
        pltpu.make_async_copy(weight_grad, weight_out, sem.at[1]),
    ]

    @pl.when(pl.program_id(0) == 0)
    def _():
        for copy in passing:
            copy.start()

    for i in range(0, band.shape[0], 2):
        wide = jnp.concatenate([flat(band[i]), flat(band[i + 1])], axis=1)
        total = mm(forward_t[...], wide)
        for side in range(2):
            part = total[:, side * half : (side + 1) * half]
            out[i + side] = (cotangent[i + side].astype(jnp.float32) + part).astype(out.dtype)

    @pl.when(pl.program_id(0) == pl.num_programs(0) - 1)
    def _():
        for copy in passing:
            copy.wait()


def final_field_grad(band, cotangent, forward_t, output, weight_grad):
    held, n, rows, half = band.shape
    longitudes = cotangent.shape[1]
    lat = pl.BlockSpec((2, longitudes, half), lambda i: (i, 0, 0))
    return pl.pallas_call(
        field_grad_kernel,
        grid=(held // 2,),
        out_shape=tuple(
            jax.ShapeDtypeStruct(like.shape, like.dtype) for like in (cotangent, output, weight_grad)
        ),
        in_specs=[
            pl.BlockSpec((2, n, rows, half), lambda i: (i, 0, 0, 0)),
            lat,
            pl.BlockSpec(forward_t.shape, lambda i: (0, 0)),
            any_spec(),
            any_spec(),
        ],
        out_specs=(lat, any_spec(), any_spec()),
        scratch_shapes=[pltpu.SemaphoreType.DMA((2,))],
        compiler_params=pltpu.CompilerParams(vmem_limit_bytes=24 * 2**20),
        name="field_grad",
    )(band, cotangent, forward_t, output, weight_grad)


def order_block(s):
    return s + ((s // 2) % 2) * (1 - 2 * (s % 2))


def holds(n, orders_at, degrees_at):
    return order_block(orders_at) + degrees_at >= n - 1


def degree_kernel(n, backward, scale, *refs):
    if backward:
        x, weights, coeffs, y, weight_grad, blocks = refs[:6]
    else:
        x, weights, y, blocks = refs[:4]
    mixed, zero, zero_sem, send1, recv1, own1, fsend, frecv, send2, recv2, own2 = refs[-11:]
    me = lax.axis_index("space")
    chan = lax.axis_index("chan")
    held, half = blocks.shape[1], blocks.shape[-1]
    mine = pl.ds(pl.multiple_of(chan * half, half), half)
    theirs = pl.ds(pl.multiple_of((1 - chan) * half, half), half)
    Exchange(n, held, False, True).greet(True)

    def ahead(k):
        return lax.rem(me + k, n)

    def behind(k):
        return lax.rem(me + n - k, n)

    def rows_of(ref, d):
        return ref.at[pl.ds(d * held, held)]

    def coming(k, sending):
        return pltpu.make_async_remote_copy(
            src_ref=rows_of(x, ahead(k)),
            dst_ref=blocks.at[0, :, me if sending else behind(k)],
            send_sem=send1.at[k],
            recv_sem=recv1.at[k],
            device_id={"space": ahead(k) if sending else behind(k)},
            device_id_type=MESH,
        )

    def across(k):
        return pltpu.make_async_remote_copy(
            src_ref=blocks.at[0, :, behind(k)],
            dst_ref=blocks.at[1, :, behind(k)],
            send_sem=fsend.at[k],
            recv_sem=frecv.at[k],
            device_id={"chan": 1 - chan},
            device_id_type=MESH,
        )

    def going(k, sending):
        return pltpu.make_async_remote_copy(
            src_ref=mixed.at[:, behind(k)],
            dst_ref=rows_of(y, me if sending else ahead(k)),
            send_sem=send2.at[k],
            recv_sem=recv2.at[k],
            device_id={"space": behind(k) if sending else ahead(k)},
            device_id_type=MESH,
        )

    def start_coming(k, carry):
        pl.when(holds(n, me, ahead(k)))(lambda: coming(k, True).start())
        return carry

    lax.fori_loop(1, n, start_coming, 0)
    own_in = pltpu.make_async_copy(rows_of(x, me), blocks.at[0, :, me], own1)
    own_out = pltpu.make_async_copy(mixed.at[:, me], rows_of(y, me), own2)
    zero[...] = jnp.zeros_like(zero)

    def zeros_of(k):
        return pltpu.make_async_copy(zero, rows_of(y, ahead(k)), zero_sem.at[k])

    def fill(k, carry):
        other = behind(k)

        @pl.when(jnp.logical_not(holds(n, other, me)))
        def _():
            for side in range(2):
                for at in range(held):
                    blocks[side, at, other] = jnp.zeros(blocks.shape[3:], blocks.dtype)

        pl.when(jnp.logical_not(holds(n, me, ahead(k))))(lambda: zeros_of(k).start())
        return carry

    def mix(other):
        for at in range(held):
            wide = jnp.concatenate([blocks[0, at, other], blocks[1, at, other]], axis=1)
            if backward:
                weight = jnp.concatenate([weights[0, at], weights[1, at]], axis=1)
                total = lax.dot_general(
                    wide, weight, (((1,), (1,)), ((), ())), preferred_element_type=jnp.float32
                )
            else:
                weight = jnp.concatenate([weights[at, mine, :], weights[at, theirs, :]], axis=0)
                total = mm(wide, weight)
            mixed[at, other] = (total * scale).astype(mixed.dtype)

    has_own = holds(n, me, me)

    @pl.when(has_own)
    def _():
        own_in.start()
        own_in.wait()
        across(0).start()

    lax.fori_loop(0, n, fill, 0)

    def settle(k):
        across(k).wait_recv()
        mix(behind(k))
        going(k, True).start()

    def turn(k, carry):
        @pl.when(holds(n, behind(k), me))
        def _():
            coming(k, False).wait_recv()
            across(k).start()

        @pl.when(jnp.logical_and(k > 1, holds(n, behind(k - 1), me)))
        def _():
            settle(k - 1)

        return carry

    lax.fori_loop(1, n, turn, 0)
    pl.when(holds(n, behind(n - 1), me))(lambda: settle(n - 1))

    @pl.when(has_own)
    def _():
        across(0).wait_recv()
        mix(me)
        own_out.start()

    if backward:

        def products(at, carry):
            grad = flat(blocks[0, at])
            for side, lines in ((0, mine), (1, theirs)):
                part = lax.dot_general(
                    flat(coeffs[side, at]),
                    grad,
                    (((0,), (0,)), ((), ())),
                    preferred_element_type=jnp.float32,
                )
                weight_grad[at, lines, :] = (part * scale).astype(weight_grad.dtype)
            return carry

        lax.fori_loop(0, held, products, 0)

    @pl.when(has_own)
    def _():
        own_out.wait()
        across(0).wait_send()

    def finish(k, carry):
        @pl.when(holds(n, behind(k), me))
        def _():
            across(k).wait_send()
            going(k, True).wait_send()

        @pl.when(holds(n, me, ahead(k)))
        def _():
            coming(k, True).wait_send()
            going(k, False).wait_recv()

        return carry

    lax.fori_loop(1, n, finish, 0)

    def filled(k, carry):
        pl.when(jnp.logical_not(holds(n, me, ahead(k))))(lambda: zeros_of(k).wait())
        return carry

    lax.fori_loop(0, n, filled, 0)


def degree_exchange(x, weights, n, scale, collective_id, coeffs=None):
    total, rows, half = x.shape
    held = total // n
    backward = coeffs is not None
    block = jax.ShapeDtypeStruct((2, held, n, rows, half), x.dtype)
    shapes = [jax.ShapeDtypeStruct(x.shape, x.dtype)]
    specs = [any_spec(), vmem_spec()]
    scratch = []
    if backward:
        shapes.append(jax.ShapeDtypeStruct((held, 2 * half, half), x.dtype))
        scratch.append(pltpu.VMEM(block.shape, x.dtype))
    else:
        shapes.append(block)
    dma = pltpu.SemaphoreType.DMA
    return pl.pallas_call(
        functools.partial(degree_kernel, n, backward, scale),
        out_shape=tuple(shapes),
        in_specs=[any_spec()] + [vmem_spec()] * (2 if backward else 1),
        out_specs=tuple(specs),
        scratch_shapes=scratch
        + [
            pltpu.VMEM((held, n, rows, half), x.dtype),
            pltpu.VMEM((held, rows, half), x.dtype),
            dma((n,)),
            dma((n,)),
            dma((n,)),
            dma,
            dma((n,)),
            dma((n,)),
            dma((n,)),
            dma((n,)),
            dma,
        ],
        compiler_params=params(collective_id),
        name="degree_exchange",
    )(*([x, weights] + ([coeffs] if backward else [])))


def dot32(formula, left, right):
    return jnp.einsum(formula, left, right, preferred_element_type=jnp.float32)


def local(field, spectral_weight, cotangent):
    n = lax.axis_size("space")
    held, longitudes, half = field.shape
    degrees_held, channels, _ = spectral_weight.shape
    latitudes = held * n
    degrees = degrees_held * n
    orders_held = degrees_held
    rows = 2 * orders_held
    mix_scale = 1.0 / math.sqrt(channels)
    chan = lax.axis_index("chan")
    held_blocks = [n - 1 - order_block(s) for s in range(n)]
    order_list = np.arange(degrees).reshape(n, orders_held)[held_blocks].reshape(-1)
    forward_np, inverse_np = fourier_tables(longitudes, order_list)
    forward, inverse = jnp.asarray(forward_np), jnp.asarray(inverse_np)
    log_np, rows_np, scale = latitude_rows(latitudes, longitudes, degrees)
    last = np.zeros((1, orders_held, latitudes), np.float32)
    last[0, :2] = rows_np
    starts = np.concatenate([log_np.reshape(n, orders_held, latitudes), last])
    by_order, analysis, synthesis, weights = fourier_exchange(
        field, spectral_weight, forward, n, rows, jnp.asarray(starts), scale, 0
    )

    def to_degrees(table, values):
        values = values.reshape(latitudes, orders_held, 2, half)
        out = dot32("mlj,jmrc->lmrc", table, values).astype(jnp.bfloat16)
        return out.reshape(degrees, rows, half)

    def to_latitudes(table, values):
        values = values.reshape(degrees, orders_held, 2, half)
        out = dot32("mlj,lmrc->jmrc", table, values).astype(jnp.bfloat16)
        return out.reshape(latitudes, rows, half)

    mixed_orders, coeffs = degree_exchange(
        to_degrees(analysis, by_order), spectral_weight, n, mix_scale, 1
    )
    output, grad_by_order = response_exchange(
        to_latitudes(synthesis, mixed_orders),
        field,
        cotangent,
        jnp.asarray(np.ascontiguousarray(inverse_np.T)),
        inverse,
        n,
        3,
    )
    coeff_orders, weight_grad = degree_exchange(
        to_degrees(synthesis, grad_by_order), weights, n, mix_scale, 5, coeffs
    )
    fourier_band = swap(to_latitudes(analysis, coeff_orders), n, False, False, 7)
    field_grad, output, weight_grad = final_field_grad(
        fourier_band,
        cotangent,
        jnp.asarray(np.ascontiguousarray(forward_np.T)),
        output,
        weight_grad,
    )
    return (output, field_grad, weight_grad)


def solution(mesh):
    in_specs = (
        P(("parts", "space"), None, "chan"),
        P("space", None, "chan"),
        P(("parts", "space"), None, "chan"),
    )
    out_specs = (
        P(("parts", "space"), None, "chan"),
        P(("parts", "space"), None, "chan"),
        P(("parts", "space"), None, "chan"),
    )
    return jax.shard_map(local, mesh=mesh, in_specs=in_specs, out_specs=out_specs, check_vma=False)
```
